128 devices in a mesh: gx: 8 (over x, core), row: 16 (over y, z).
Axes of the slice: x: 4, y: 4, z: 4, core: 2. Of those that a mesh axis runs over, the one named last changes fastest.
Arguments:
- eddy_fields: float32 [5, 64, 512, 256], P(None, 'gx', 'row'), may hold values from -0.6 to 0.6, as said below
- acoustic_fields: float32 [4, 128, 256, 256], P(None, 'gx', 'row'), may hold values from -1.2 to 1.2
- weights: bfloat16 [8, 16, 128, 128, 128], P('gx', 'row'), may hold values from -0.5 to 0.5
- source_block: int32 [8, 16, 128], P('gx', 'row'), may hold values from 0 to 511
- target_device: int32 [8, 16, 128, 1], P('gx', 'row'), may hold values from 0 to 127; in each aligned block of 128 rows (0 to 127, 128 to 255, ..., all dimensions but the last counted through in order) at most 2 rows name the same one
- target_block: int32 [8, 16, 128], P('gx', 'row'), may hold values from 0 to 511
- live_count: int32 [8, 16], P('gx', 'row'), may hold values from 64 to 128, as said below
Outputs:
- eddy_next: float32 [5, 64, 512, 256], P(None, 'gx', 'row')
- acoustic_next: float32 [4, 128, 256, 256], P(None, 'gx', 'row')
The draws below stay inside these ranges and needn't reach their ends.
Inputs may be any that keep to these rules, and one draw needn't show every extreme that they name: `eddy_fields`: channel 0 (density excess) lies within -0.2 to 0.2; the other channels within -0.6 to 0.6. `target_device`: at most 2 of a device's 128 listed entries name one target device, and some device reaches that. `live_count`: at least half of each list is live, and some device has all 128 live.
All inputs are finite; a program needn't handle non-finite values.
Results may differ from the reference program's by a relative error of at most 0.0003.
Values sent between devices are 32-bit elements; how exact they have to be, the bound alone decides.
A program may use at most 192 MiB of HBM per device.

```python
import math
import jax
import jax.numpy as jnp
import numpy as np
from jax import lax

LZ = 256
CX = 16
CR = 16
CZ = 256
BLK = 128
KMAX = 128
NXL = 64
NRL = 512
NXC = 128
NRC = 256
NB_LES = 512
NB_CAA = 512
CAP = 2
N_GX = 8
N_ROW = 16
DEVICES = 128


def draw_eddy_fields(key, part):
    key = jax.random.fold_in(key, 11)
    first_key, second_key = jax.random.split(key)
    density_part = jnp.clip(0.07 * jax.random.normal(first_key, (1, NXL, NRL, LZ), jnp.float32), -0.2, 0.2)
    other_part = jnp.clip(0.15 * jax.random.normal(second_key, (4, NXL, NRL, LZ), jnp.float32), -0.6, 0.6)
    return jnp.concatenate([density_part, other_part], 0).astype(jnp.float32)


def draw_live_count(key, part):
    key = jax.random.fold_in(key, 7)
    first_key, second_key = jax.random.split(key)
    totals = jax.random.randint(first_key, (N_GX * N_ROW,), KMAX // 2, KMAX + 1)
    chosen = jax.random.randint(second_key, (), 0, N_GX * N_ROW)
    totals = jnp.where(jnp.arange(N_GX * N_ROW) == chosen, KMAX, totals)
    return totals.reshape(N_GX, N_ROW).astype(jnp.int32)


def touch_ends(array, own_key, least, largest):
    shape = array.shape
    place = [jax.random.randint(jax.random.fold_in(own_key, axis), (), 0, shape[axis]) for axis in range(len(shape))]
    array = array.at[tuple(place)].set(least)
    longest = shape.index(max(shape))
    place[longest] = (place[longest] + 1) % shape[longest]
    return array.at[tuple(place)].set(largest)


def shard_levels(rng, shape, shards, low, largest):
    factor_of = 1.0
    for dim, parts in shards:
        heights = jax.random.uniform(jax.random.fold_in(jax.random.fold_in(rng, 6), dim), (parts,), jnp.float32, low / len(shards), largest / len(shards))
        factor_of = factor_of * jnp.repeat(jnp.exp(heights), shape[dim] // parts).reshape((-1,) + (1,) * (len(shape) - 1 - dim))
    return factor_of


def deal_out(own_key, own, number, rows, count, top, limit, slope):
    sequence = jax.random.permutation(own_key, count)
    heavy_load, usual = load_shares(count, rows * top, limit, slope, True), load_shares(count, rows * top, limit, slope, False)
    places = jnp.arange(count)

    def named(tallies, turn):
        used = int((tallies > 0).sum())
        fixed = max(1, used // 4)
        shifted = fixed + (places - fixed + turn * (used - fixed)) % max(1, count - fixed)
        return jnp.zeros((count,), jnp.int32).at[sequence[jnp.where(places < fixed, places, shifted)]].set(jnp.asarray(tallies, jnp.int32))

    tallies = jnp.where(number % 4 == 0, named(heavy_load, number // 4), named(usual, number - number // 4 - 1))
    mixed = jax.random.permutation(jax.random.fold_in(own, 3), count)
    donor, receiver = mixed[0:count // 2 * 2:2], mixed[1:count // 2 * 2:2]
    room = jnp.minimum(tallies[donor] - 1, limit - tallies[receiver]) // 2
    room = jnp.where((donor == sequence[0]) | (receiver == sequence[0]) | (tallies[receiver] == 0), 0, jnp.maximum(room, 0))
    shifted = jax.random.randint(jax.random.fold_in(own, 4), (count // 2,), 0, 1 << 20) % (room + 1)
    tallies = tallies.at[donor].add(-shifted).at[receiver].add(shifted)
    labels = jnp.searchsorted(jnp.cumsum(tallies), jnp.arange(rows * top), side="right").astype(jnp.int32)
    listing = labels.reshape(top, rows).T
    listing = listing[jax.random.permutation(jax.random.fold_in(own, 1), rows)]
    turn = jax.random.randint(jax.random.fold_in(own, 2), (rows, 1), 0, top)
    return jnp.take_along_axis(listing, (jnp.arange(top)[None, :] + turn) % top, axis=1)


def load_shares(number_of, total, reach, skew, full):
    loads = [(1 << 20) // math.isqrt(rank ** skew) + 1 for rank in range(1, number_of + 1)]
    largest = reach if full else min(reach, max(-(-total // number_of), total * loads[0] // sum(loads)))
    least = 1 if total - largest >= number_of - 1 else 0
    counts, rest = [largest] + [least] * (number_of - 1), total - largest - least * (number_of - 1)
    while rest > 0:
        movable = [i for i in range(1, number_of) if counts[i] < largest] or [i for i in range(1, number_of) if counts[i] < reach]
        mass, remaining = sum([loads[i] for i in movable]), rest
        for i in movable:
            extra = min(reach - counts[i], max(1, remaining * loads[i] // mass), rest)
            counts[i] = counts[i] + extra
            rest = rest - extra
    return np.array(counts)


def centred(key, extent, spread, reach, cuts=(), kind=jnp.bfloat16):
    factor_of = shard_levels(key, extent, cuts, -0.22, 0.18) if cuts else 1.0
    array = jax.random.normal(key, extent, jnp.float32) * spread * factor_of
    return jnp.minimum(jnp.maximum(array, -reach), reach).astype(kind)


def setup_inputs(seed: int = 0) -> dict:
    key_of = jax.random.split(jax.random.key(seed), 8)
    eddy_fields = draw_eddy_fields(jax.random.fold_in(key_of[7], 71), 0)
    acoustic_fields = centred(key_of[1], (4, NXC, NRC, CZ), 0.2, 1.2, ((1, 8), (2, 16)), jnp.float32)
    weights = centred(key_of[2], (N_GX, N_ROW, KMAX, BLK, BLK), BLK ** -0.5, 0.5, ((0, 8), (1, 16)))
    source_block = touch_ends(jax.random.randint(key_of[3], (N_GX, N_ROW, KMAX), 0, NB_LES), jax.random.fold_in(key_of[3], 1), 0, NB_LES - 1).astype(jnp.int32)
    target_device_keys = jax.random.split(jax.random.fold_in(key_of[4], 1), N_GX * N_ROW * KMAX // KMAX)
    target_device_turns = jax.random.permutation(jax.random.fold_in(key_of[4], 3), N_GX * N_ROW * KMAX // KMAX)
    target_device = jax.vmap(lambda own, number: deal_out(jax.random.fold_in(key_of[4], 2), own, number, KMAX, DEVICES, 1, CAP, 2))(target_device_keys, target_device_turns).reshape((N_GX, N_ROW, KMAX, 1))
    target_block = touch_ends(jax.random.randint(key_of[5], (N_GX, N_ROW, KMAX), 0, NB_CAA), jax.random.fold_in(key_of[5], 1), 0, NB_CAA - 1).astype(jnp.int32)
    live_count = draw_live_count(jax.random.fold_in(key_of[7], 71), 0)
    return {"eddy_fields": eddy_fields, "acoustic_fields": acoustic_fields, "weights": weights, "source_block": source_block, "target_device": target_device, "target_block": target_block, "live_count": live_count}


gamma_gas = 1.4
viscosity = 0.5
eddy_timestep = 0.2
sound_timestep = 0.5
mean_mach = 0.3
stencil_one = 0.75
stencil_two = -0.15
stencil_three = 1.0 / 60.0


def eddy_update(padded):
    middle = padded[:, 1:-1, 1:-1, :]
    grad_x = 0.5 * (padded[:, 2:, 1:-1, :] - padded[:, :-2, 1:-1, :])
    grad_r = 0.5 * (padded[:, 1:-1, 2:, :] - padded[:, 1:-1, :-2, :])
    upper_z = jnp.roll(middle, -1, axis=3)
    lower_z = jnp.roll(middle, 1, axis=3)
    grad_z = 0.5 * (upper_z - lower_z)
    laplace = padded[:, 2:, 1:-1, :] + padded[:, :-2, 1:-1, :] + padded[:, 1:-1, 2:, :] + padded[:, 1:-1, :-2, :] + upper_z + lower_z - 6.0 * middle
    flow_x, flow_r, flow_z = middle[1], middle[2], middle[3]
    advect = flow_x * grad_x + flow_r * grad_r + flow_z * grad_z
    divergence = grad_x[1] + grad_r[2] + grad_z[3]
    density = 1.0 + middle[0]
    pressure = 1.0 / gamma_gas + middle[4]
    forcing = jnp.stack([density * divergence, grad_x[4] / density, grad_r[4] / density, grad_z[4] / density, gamma_gas * pressure * divergence])
    return middle + eddy_timestep * (viscosity * laplace - advect - forcing)


def eddy_sources(fields):
    density = 1.0 + fields[0]
    return jnp.stack([fields[4], density * fields[1], density * fields[2], density * fields[3]]).astype(jnp.bfloat16)


def acoustic_tendency(padded, source):
    size_x = padded.shape[1] - 6
    size_r = padded.shape[2] - 6
    middle = padded[:, 3:3 + size_x, 3:3 + size_r, :]

    def along_x(shift):
        return padded[:, 3 + shift:3 + shift + size_x, 3:3 + size_r, :] - padded[:, 3 - shift:3 - shift + size_x, 3:3 + size_r, :]

    def along_r(shift):
        return padded[:, 3:3 + size_x, 3 + shift:3 + shift + size_r, :] - padded[:, 3:3 + size_x, 3 - shift:3 - shift + size_r, :]

    def along_z(shift):
        return jnp.roll(middle, -shift, axis=3) - jnp.roll(middle, shift, axis=3)

    grad_x = stencil_one * along_x(1) + stencil_two * along_x(2) + stencil_three * along_x(3)
    grad_r = stencil_one * along_r(1) + stencil_two * along_r(2) + stencil_three * along_r(3)
    grad_z = stencil_one * along_z(1) + stencil_two * along_z(2) + stencil_three * along_z(3)
    rate_p = -(mean_mach * grad_x[0] + grad_x[1] + grad_r[2] + grad_z[3]) + source[0]
    rate_u = -(mean_mach * grad_x[1] + grad_x[0]) + source[1]
    rate_v = -(mean_mach * grad_x[2] + grad_r[0]) + source[2]
    rate_w = -(mean_mach * grad_x[3] + grad_z[0]) + source[3]
    return jnp.stack([rate_p, rate_u, rate_v, rate_w])


def runge_step(fields, source, pad_field):
    slope_one = acoustic_tendency(pad_field(fields), source)
    slope_two = acoustic_tendency(pad_field(fields + (0.5 * sound_timestep) * slope_one), source)
    slope_three = acoustic_tendency(pad_field(fields + (0.5 * sound_timestep) * slope_two), source)
    slope_four = acoustic_tendency(pad_field(fields + sound_timestep * slope_three), source)
    return fields + (sound_timestep / 6.0) * (slope_one + 2.0 * slope_two + 2.0 * slope_three + slope_four)


def into_blocks(field, parts_x, parts_r):
    channels, size_x, size_r, size_z = field.shape
    cells_x = size_x // parts_x
    cells_r = size_r // parts_r
    moved = field.reshape(channels, parts_x, cells_x, parts_r, cells_r, size_z).transpose(1, 3, 0, 2, 4, 5)
    return moved.reshape(parts_x, parts_r, channels, cells_x * cells_r * size_z // BLK, BLK)


def from_blocks(blocks, cells_x, cells_r, size_z):
    parts_x, parts_r, channels = blocks.shape[0], blocks.shape[1], blocks.shape[2]
    moved = blocks.reshape(parts_x, parts_r, channels, cells_x, cells_r, size_z).transpose(2, 0, 3, 1, 4, 5)
    return moved.reshape(channels, parts_x * cells_x, parts_r * cells_r, size_z)


def pad_three(field):
    return jnp.pad(field, ((0, 0), (3, 3), (3, 3), (0, 0)))


def reference(eddy_fields, acoustic_fields, weights, source_block, target_device, target_block, live_count):
    fields = eddy_fields
    for sweep in range(2):
        fields = eddy_update(jnp.pad(fields, ((0, 0), (1, 1), (1, 1), (0, 0))))
    sources = eddy_sources(fields)
    source_blocks = into_blocks(sources, N_GX, N_ROW).reshape(N_GX * N_ROW, 4, NB_LES, BLK)
    matrices_all = weights.reshape(N_GX * N_ROW, KMAX, BLK, BLK)

    def one_device(packed):
        blocks, matrices, picks, alive_total = packed
        picked = jnp.take(blocks, picks, axis=1).astype(jnp.float32)
        contribution = jnp.einsum('kij,ckj->kci', matrices.astype(jnp.float32), picked)
        is_live = jnp.arange(KMAX) < alive_total
        return jnp.where(is_live[:, None, None], contribution, 0.0)

    contributions = lax.map(one_device, (source_blocks, matrices_all, source_block.reshape(N_GX * N_ROW, KMAX), live_count.reshape(N_GX * N_ROW)))
    target = jnp.zeros((N_GX * N_ROW, NB_CAA, 4, BLK), jnp.float32)
    target = target.at[target_device.reshape(-1), target_block.reshape(-1)].add(contributions.reshape(N_GX * N_ROW * KMAX, 4, BLK))
    acoustic_source = from_blocks(target.transpose(0, 2, 1, 3).reshape(N_GX, N_ROW, 4, NB_CAA, BLK), CX, CR, CZ)
    acoustic_next = runge_step(acoustic_fields, acoustic_source, pad_three)
    return fields, acoustic_next
```

```python
import functools

import jax
import jax.numpy as jnp
from jax import lax
from jax.experimental import pallas as pl
from jax.experimental.pallas import tpu as pltpu
from jax.sharding import PartitionSpec as P

MESH = pl.DeviceIdType.MESH
F32 = jnp.float32

gamma_gas = 1.4
sound_timestep = 0.5
mean_mach = 0.3
stencil = (0.75, -0.15, 1.0 / 60.0)

GX = 8
ROW = 16
DEV = GX * ROW
FR = 48
AR = 32
CORNERS = ((0, 0), (0, 1), (1, 0), (1, 1))
RADIAL = (0, 2)


def shifted(low, high, lane, step):
    if step > 0:
        a, b = pltpu.roll(low, 128 - step, 1), pltpu.roll(high, 128 - step, 1)
        keep = lane < 128 - step
    else:
        a, b = pltpu.roll(low, -step, 1), pltpu.roll(high, -step, 1)
        keep = lane >= -step
    return jnp.where(keep, a, b), jnp.where(keep, b, a)


def flow_tile(src, x, row, lane, emit):
    rows = pl.ds(row, 8)
    center = [[src[c, x, zh, rows, :] for zh in range(2)] for c in range(5)]
    upper = [shifted(center[c][0], center[c][1], lane, 1) for c in range(5)]
    lower = [shifted(center[c][0], center[c][1], lane, -1) for c in range(5)]
    for zh in range(2):
        dx, dr, dz, lap = [], [], [], []
        for c in range(5):
            xp, xm = src[c, x + 1, zh, rows, :], src[c, x - 1, zh, rows, :]
            rp, rm = src[c, x, zh, pl.ds(row + 1, 8), :], src[c, x, zh, pl.ds(row - 1, 8), :]
            zp, zm = upper[c][zh], lower[c][zh]
            dx.append(xp - xm)
            dr.append(rp - rm)
            dz.append(zp - zm)
            lap.append(((xp + xm) + (rp + rm)) + ((zp + zm) - 6.0 * center[c][zh]))
        q = [center[c][zh] for c in range(5)]
        div = dx[1] + dr[2] + dz[3]
        rho = 1.0 + q[0]
        inv = 1.0 / rho
        force = (
            rho * div,
            dx[4] * inv,
            dr[4] * inv,
            dz[4] * inv,
            (gamma_gas * q[4] + 1.0) * div,
        )
        new = []
        for c in range(5):
            adv = q[1] * dx[c] + q[2] * dr[c] + q[3] * dz[c]
            new.append(q[c] + 0.1 * (lap[c] - adv - force[c]))
        emit(zh, new)


def rate_tile(src, x, row, lane):
    rows = pl.ds(row, 8)

    def grad_x(c, zh):
        total = None
        for k in range(3):
            part = stencil[k] * (src[c, x + 4 + k, zh, rows, :] - src[c, x + 2 - k, zh, rows, :])
            total = part if total is None else total + part
        return total

    def grad_r(c, zh):
        total = None
        for k in range(3):
            part = stencil[k] * (
                src[c, x + 3, zh, pl.ds(row + k + 1, 8), :]
                - src[c, x + 3, zh, pl.ds(row - k - 1, 8), :]
            )
            total = part if total is None else total + part
        return total

    def grad_z(c):
        low, high = src[c, x + 3, 0, rows, :], src[c, x + 3, 1, rows, :]
        total = None
        for k in range(3):
            up = shifted(low, high, lane, k + 1)
            down = shifted(low, high, lane, -k - 1)
            part = [stencil[k] * (up[zh] - down[zh]) for zh in range(2)]
            total = part if total is None else [total[zh] + part[zh] for zh in range(2)]
        return total

    zp, zw = grad_z(0), grad_z(3)
    out = []
    for zh in range(2):
        xp, xu, xv, xw = (grad_x(c, zh) for c in range(4))
        out.append(
            (
                -(mean_mach * xp + xu + grad_r(2, zh) + zw[zh]),
                -(mean_mach * xu + xp),
                -(mean_mach * xv + grad_r(0, zh)),
                -(mean_mach * xw + zp[zh]),
            )
        )
    return out


def kernel(
    eddy, acoustic, weights, target, tblock, sblock, live, eddy_out, acoustic_out,
    f0, f1, f2, srcs, wv, contrib, outgoing, incoming, ys, rsend, rrecv, fsend, frecv, csend, crecv,
    lists, square, turned, slots, slots_s, onehot, source, base, final,
    load_sem, slot_sem, fx_s, fx_r, fr_s, fr_r, fc_s, fc_r, l1_s, l1_r, l2_s, l2_r, aa_s, aa_r,
    ax_s, ax_r, ar_s, ar_r, out_sem,
):
    g, r = lax.axis_index("gx"), lax.axis_index("row")
    me = g * ROW + r
    left, right = lax.rem(g + GX - 1, GX), lax.rem(g + 1, GX)
    below, above = lax.rem(r + ROW - 1, ROW), lax.rem(r + 1, ROW)
    lane = lax.broadcasted_iota(jnp.int32, (8, 128), 1)
    sub = lax.broadcasted_iota(jnp.int32, (8, 128), 0)

    def remote(src, dst, send, recv, where):
        return pltpu.make_async_remote_copy(
            src_ref=src, dst_ref=dst, send_sem=send, recv_sem=recv, device_id=where, device_id_type=MESH
        )

    bar = pltpu.get_barrier_semaphore()

    @pl.loop(1, ROW)
    def _(k):
        pl.semaphore_signal(bar, inc=1, device_id=(g, lax.rem(r + k, ROW)), device_id_type=MESH)

    @pl.loop(1, GX)
    def _(k):
        pl.semaphore_signal(bar, inc=1, device_id=(lax.rem(g + k, GX), r), device_id_type=MESH)

    for i, j in CORNERS:
        where = ((left, right)[i], (below, above)[j])
        pl.semaphore_signal(bar, inc=1, device_id=where, device_id_type=MESH)

    loads = []
    for zh in range(2):
        lanes = pl.ds(128 * zh, 128)
        loads.append(
            pltpu.make_async_copy(
                eddy.at[:, :, :, lanes], f0.at[:, pl.ds(2, 8), zh, pl.ds(8, 32), :], load_sem.at[zh]
            )
        )
    for zh in range(2):
        lanes = pl.ds(128 * zh, 128)
        loads.append(
            pltpu.make_async_copy(
                acoustic.at[:, :, :, lanes],
                ys.at[0, :, pl.ds(3, 16), zh, pl.ds(8, 16), :],
                load_sem.at[2 + zh],
            )
        )
    loads.append(pltpu.make_async_copy(weights, wv, load_sem.at[4]))
    for copy in loads:
        copy.start()

    entry = lax.broadcasted_iota(jnp.int32, (128, 128), 0)
    device = lax.broadcasted_iota(jnp.int32, (128, 128), 1)
    named = jnp.broadcast_to(target[...], (128, 128)).T
    block = jnp.broadcast_to(tblock[...], (128, 128)).T
    hit = (named == device) & (entry < live[0])
    first = jnp.min(jnp.where(hit, entry, 128), axis=0, keepdims=True)
    last = jnp.max(jnp.where(hit, entry, -1), axis=0, keepdims=True)
    id_first = jnp.max(jnp.where(hit & (entry == first), block, -1), axis=0, keepdims=True)
    id_last = jnp.max(jnp.where(hit & (entry == last), block, -1), axis=0, keepdims=True)
    slots[0:1, :] = jnp.where(first < 128, first, 0)
    slots[1:2, :] = jnp.maximum(last, 0)
    lists[me, 0:1, :] = id_first
    lists[me, 1:2, :] = jnp.where(last > first, id_last, -1)
    slot_copy = pltpu.make_async_copy(slots, slots_s, slot_sem)
    slot_copy.start()

    zero = jnp.zeros((8, 128), F32)

    @pl.when(r == 0)
    def _():
        f0[:, :, :, 0:8, :] = jnp.zeros((5, 12, 2, 8, 128), F32)

        @pl.loop(0, 4)
        def _(n):
            ys[n, :, :, :, 0:8, :] = jnp.zeros((4, 22, 2, 8, 128), F32)

    @pl.when(r == ROW - 1)
    def _():
        f0[:, :, :, 40:48, :] = jnp.zeros((5, 12, 2, 8, 128), F32)

        @pl.loop(0, 4)
        def _(n):
            ys[n, :, :, :, 24:32, :] = jnp.zeros((4, 22, 2, 8, 128), F32)

    loads[0].wait()
    loads[1].wait()

    flat0 = f0.reshape(5 * 12 * 2 * FR, 128)

    def flow_row(c, x, zh, row):
        return ((c * 12 + x) * 2 + zh) * FR + row

    for side in range(2):
        for c in range(5):
            for k in range(2):
                for zh in range(2):
                    start = flow_row(c, 2, zh, (8, 38)[side] + k)
                    fsend[side, (c * 2 + k) * 2 + zh] = flat0[pl.ds(start, 8, stride=2 * FR), :]
    for n, (i, j) in enumerate(CORNERS):
        for c in range(5):
            for zh in range(2):
                start = flow_row(c, (2, 9)[i], zh, (8, 39)[j])
                csend[n, 2 * c + zh : 2 * c + zh + 1, :] = flat0[pl.ds(start, 1), :]

    pl.semaphore_wait(bar, ROW - 1 + GX - 1 + 4)

    flow_copies = [
        remote(fsend.at[0], frecv.at[0], fr_s.at[0], fr_r.at[0], (g, below)),
        remote(fsend.at[1], frecv.at[1], fr_s.at[1], fr_r.at[1], (g, above)),
    ]
    for n, (i, j) in enumerate(CORNERS):
        where = ((left, right)[i], (below, above)[j])
        flow_copies.append(remote(csend.at[n], crecv.at[n], fc_s.at[n], fc_r.at[n], where))
    inner = pl.ds(8, 32)
    flow_copies.append(
        remote(
            f0.at[:, pl.ds(2, 2), :, inner, :], f0.at[:, pl.ds(10, 2), :, inner, :],
            fx_s.at[0], fx_r.at[0], (left, r),
        )
    )
    flow_copies.append(
        remote(
            f0.at[:, pl.ds(8, 2), :, inner, :], f0.at[:, pl.ds(0, 2), :, inner, :],
            fx_s.at[1], fx_r.at[1], (right, r),
        )
    )
    for copy in flow_copies:
        copy.start()

    @pl.loop(1, ROW)
    def _(k):
        remote(lists.at[me], lists.at[me], l1_s, l1_r, (g, lax.rem(r + k, ROW))).start()

    def first_step(x, tiles):
        for t in tiles:
            row = 7 + 8 * t

            def emit(zh, new):
                for c in range(5):
                    f1[c, x - 1, zh, pl.ds(row, 8), :] = new[c]

            flow_tile(f0, x, row, lane, emit)

    @pl.loop(3, 9)
    def _(x):
        first_step(x, (1, 2, 3))

    flow_copies[0].wait_recv()
    flow_copies[1].wait_recv()

    def unpack_flow(side):
        for c in range(5):
            for k in range(2):
                for zh in range(2):
                    start = flow_row(c, 2, zh, (40, 6)[side] + k)
                    flat0[pl.ds(start, 8, stride=2 * FR), :] = frecv[side, (c * 2 + k) * 2 + zh]

    @pl.when(r < ROW - 1)
    def _():
        unpack_flow(0)

    @pl.when(r > 0)
    def _():
        unpack_flow(1)

    @pl.loop(3, 9)
    def _(x):
        first_step(x, (0, 4))

    for copy in flow_copies[2:]:
        copy.wait_recv()
    pltpu.make_async_copy(lists.at[pl.ds(0, ROW - 1)], lists.at[pl.ds(0, ROW - 1)], l1_r).wait()
    plane = lists.at[pl.ds(g * ROW, ROW)]

    @pl.loop(1, GX)
    def _(k):
        remote(plane, plane, l2_s, l2_r, (lax.rem(g + k, GX), r)).start()

    for n, (i, j) in enumerate(CORNERS):

        @pl.when(jnp.logical_and((g < GX - 1, g > 0)[i], (r < ROW - 1, r > 0)[j]))
        def _():
            for c in range(5):
                for zh in range(2):
                    start = flow_row(c, (10, 1)[i], zh, (40, 7)[j])
                    flat0[pl.ds(start, 1), :] = crecv[n, 2 * c + zh : 2 * c + zh + 1, :]

    @pl.when(g == 0)
    def _():
        f0[:, 0:2, :, :, :] = jnp.zeros((5, 2, 2, FR, 128), F32)

    @pl.when(g == GX - 1)
    def _():
        f0[:, 10:12, :, :, :] = jnp.zeros((5, 2, 2, FR, 128), F32)

    @pl.loop(0, 4)
    def _(n):
        first_step(n + 1 + 6 * lax.div(n, 2), range(5))

    @pl.when(g == 0)
    def _():
        f1[:, 0, :, :, :] = jnp.zeros((5, 2, FR, 128), F32)

    @pl.when(g == GX - 1)
    def _():
        f1[:, 9, :, :, :] = jnp.zeros((5, 2, FR, 128), F32)

    @pl.when(r == 0)
    def _():
        f1[:, :, :, 7:8, :] = jnp.zeros((5, 10, 2, 1, 128), F32)

    @pl.when(r == ROW - 1)
    def _():
        f1[:, :, :, 40:41, :] = jnp.zeros((5, 10, 2, 1, 128), F32)

    flats = ys.reshape(4 * 4 * 22 * 2 * AR, 128)
    points = pl.ds(8, 16)

    def acoustic_row(n, c, x, zh, row):
        return (((n * 4 + c) * 22 + x) * 2 + zh) * AR + row

    def acoustic_send(n):
        for side in range(2):
            for m, c in enumerate(RADIAL):
                for k in range(3):
                    for zh in range(2):
                        for half in range(2):
                            start = acoustic_row(n, c, 3 + 8 * half, zh, (8, 21)[side] + k)
                            rsend[n, side, (m * 3 + k) * 2 + zh, 8 * half : 8 * half + 8, :] = flats[
                                pl.ds(start, 8, stride=2 * AR), :
                            ]
        copies = [
            remote(rsend.at[n, 0], rrecv.at[n, 0], ar_s.at[n, 0], ar_r.at[n, 0], (g, below)),
            remote(rsend.at[n, 1], rrecv.at[n, 1], ar_s.at[n, 1], ar_r.at[n, 1], (g, above)),
            remote(
                ys.at[n, :, pl.ds(3, 3), :, points, :], ys.at[n, :, pl.ds(19, 3), :, points, :],
                ax_s.at[n, 0], ax_r.at[n, 0], (left, r),
            ),
            remote(
                ys.at[n, :, pl.ds(16, 3), :, points, :], ys.at[n, :, pl.ds(0, 3), :, points, :],
                ax_s.at[n, 1], ax_r.at[n, 1], (right, r),
            ),
        ]
        for copy in copies:
            copy.start()
        return copies

    def acoustic_receive(n, copies):
        for copy in copies:
            copy.wait_recv()

        def unpack(side):
            for m, c in enumerate(RADIAL):
                for k in range(3):
                    for zh in range(2):
                        for half in range(2):
                            start = acoustic_row(n, c, 3 + 8 * half, zh, (24, 5)[side] + k)
                            flats[pl.ds(start, 8, stride=2 * AR), :] = rrecv[
                                n, side, (m * 3 + k) * 2 + zh, 8 * half : 8 * half + 8, :
                            ]

        @pl.when(r < ROW - 1)
        def _():
            unpack(0)

        @pl.when(r > 0)
        def _():
            unpack(1)

        @pl.when(g == 0)
        def _():
            ys[n, :, 0:3, :, 8:24, :] = jnp.zeros((4, 3, 2, 16, 128), F32)

        @pl.when(g == GX - 1)
        def _():
            ys[n, :, 19:22, :, 8:24, :] = jnp.zeros((4, 3, 2, 16, 128), F32)

    loads[2].wait()
    loads[3].wait()
    sent = [acoustic_send(0)]

    @pl.loop(0, 8)
    def _(x):
        for t in range(4):

            def emit(zh, new):
                for c in range(5):
                    f2[c, x, zh, 8 * t : 8 * t + 8, :] = new[c]
                rho = 1.0 + new[0]
                for c, value in enumerate((new[4], rho * new[1], rho * new[2], rho * new[3])):
                    srcs[pl.ds(8 + x * 256 + 64 * t + 4 * zh + c, 8, stride=8), :] = value

            flow_tile(f1, x + 1, 8 + 8 * t, lane, emit)

    out_copies = []
    for zh in range(2):
        lanes = pl.ds(128 * zh, 128)
        out_copies.append(
            pltpu.make_async_copy(f2.at[:, :, zh, :, :], eddy_out.at[:, :, :, lanes], out_sem.at[zh])
        )
        out_copies[-1].start()

    loads[4].wait()

    @pl.loop(0, 8)
    def _(m):
        for u in range(8):
            p = m * 8 + u
            low = srcs[pl.ds(8 + 4 * sblock[2 * p], 8), :]
            high = srcs[pl.ds(4 + 4 * sblock[2 * p + 1], 8), :]
            lhs = jnp.concatenate(
                [jnp.where(sub < 4, low, 0.0), jnp.where(sub < 4, 0.0, high)], axis=1
            ).astype(jnp.bfloat16)
            rhs = jnp.concatenate([wv[2 * p], wv[2 * p + 1]], axis=1)
            contrib[pl.ds(8 + 8 * p, 8), :] = lax.dot_general(
                lhs, rhs, (((1,), (1,)), ((), ())), preferred_element_type=F32
            )

    slot_copy.wait()
    rest = pl.ds(0, DEV - ROW)
    pltpu.make_async_copy(lists.at[rest], lists.at[rest], l2_r).wait()

    def slot_tile(d):
        low = contrib[pl.ds(8 + 4 * jnp.clip(slots_s[0, d], 0, 127), 8), :]
        high = contrib[pl.ds(4 + 4 * jnp.clip(slots_s[1, d], 0, 127), 8), :]
        return jnp.where(sub < 4, low, high)

    @pl.loop(1, DEV)
    def _(k):
        d = lax.rem(me + k, DEV)
        outgoing[d] = slot_tile(d)
        where = (lax.div(d, ROW), lax.rem(d, ROW))
        remote(outgoing.at[d], incoming.at[me], aa_s, aa_r, where).start()

    incoming[me] = slot_tile(me)

    @pl.loop(0, DEV)
    def _(j):
        for k in range(2):
            square[k, pl.ds(j, 1), :] = lists[j, k : k + 1, :]

    for k in range(2):
        turned[k] = square[k].T
    ids = [turned[k, pl.ds(me, 1), :] for k in range(2)]

    @pl.loop(0, 16)
    def _(x):
        place = lax.broadcasted_iota(jnp.int32, (32, 128), 0)
        place = (x * 16 + lax.rem(place, 16)) * 2 + lax.div(place, 16)
        for k in range(2):
            onehot[pl.ds(pl.multiple_of(x * 32, 32), 32), 128 * k : 128 * k + 128] = jnp.where(
                place == ids[k], 1.0, 0.0
            ).astype(jnp.bfloat16)

    acoustic_receive(0, sent[0])

    @pl.loop(0, 16)
    def _(x):
        for t in range(2):
            rate = rate_tile(ys.at[0], x, 8 + 8 * t, lane)
            for zh in range(2):
                for c in range(4):
                    old = ys[0, c, x + 3, zh, 8 + 8 * t : 16 + 8 * t, :]
                    base[c, x, zh, 8 * t : 8 * t + 8, :] = old + (sound_timestep / 4.0) * rate[zh][c]

    others = pl.ds(0, DEV - 1)
    pltpu.make_async_copy(incoming.at[others], incoming.at[others], aa_r).wait()

    flat_in = incoming.reshape((DEV + 1) * 8, 128)
    for pair in range(2):
        value = jnp.concatenate(
            [
                jnp.concatenate(
                    [flat_in[pl.ds(4 * k + 2 * pair + c, DEV, stride=8), :] for k in range(2)], axis=0
                )
                for c in range(2)
            ],
            axis=1,
        )
        high = value.astype(jnp.bfloat16)
        low = (value - high.astype(F32)).astype(jnp.bfloat16)

        @pl.loop(0, 4)
        def _(q):
            rows = onehot[pl.ds(pl.multiple_of(q * 128, 128), 128), :]
            total = jnp.dot(rows, high, preferred_element_type=F32) + jnp.dot(
                rows, low, preferred_element_type=F32
            )
            for c in range(2):
                source[2 * pair + c, pl.ds(pl.multiple_of(q * 128, 128), 128), :] = total[
                    :, 128 * c : 128 * c + 128
                ]

    def source_tile(c, x, zh, t):
        return source[c, pl.ds(pl.multiple_of(x * 32 + zh * 16 + 8 * t, 8), 8), :]

    @pl.loop(0, 16)
    def _(x):
        for t in range(2):
            for zh in range(2):
                for c in range(4):
                    ys[1, c, x + 3, zh, 8 + 8 * t : 16 + 8 * t, :] = (
                        base[c, x, zh, 8 * t : 8 * t + 8, :]
                        + (sound_timestep / 4.0) * source_tile(c, x, zh, t)
                    )

    for n in range(1, 4):
        sent.append(acoustic_send(n))
        acoustic_receive(n, sent[n])
        step = sound_timestep / (4 - n)

        @pl.loop(0, 16)
        def _(x):
            for t in range(2):
                rate = rate_tile(ys.at[n], x, 8 + 8 * t, lane)
                for zh in range(2):
                    for c in range(4):
                        old = ys[0, c, x + 3, zh, 8 + 8 * t : 16 + 8 * t, :]
                        new = old + step * (rate[zh][c] + source_tile(c, x, zh, t))
                        if n < 3:
                            ys[n + 1, c, x + 3, zh, 8 + 8 * t : 16 + 8 * t, :] = new
                        else:
                            final[c, x, zh, 8 * t : 8 * t + 8, :] = new

    for zh in range(2):
        lanes = pl.ds(128 * zh, 128)
        out_copies.append(
            pltpu.make_async_copy(
                final.at[:, :, zh, :, :], acoustic_out.at[:, :, :, lanes], out_sem.at[2 + zh]
            )
        )
        out_copies[-1].start()

    for copy in flow_copies:
        copy.wait_send()
    for copies in sent:
        for copy in copies:
            copy.wait_send()
    pltpu.make_async_copy(lists.at[pl.ds(0, ROW - 1)], lists.at[pl.ds(0, ROW - 1)], l1_s).wait()
    pltpu.make_async_copy(lists.at[rest], lists.at[rest], l2_s).wait()
    pltpu.make_async_copy(outgoing.at[others], outgoing.at[others], aa_s).wait()
    for copy in out_copies:
        copy.wait()


def body(eddy, acoustic, weights, source_block, target_device, target_block, live_count):
    vmem, dma = pltpu.VMEM, pltpu.SemaphoreType.DMA
    anywhere = pl.BlockSpec(memory_space=pl.ANY)
    in_vmem = pl.BlockSpec(memory_space=pltpu.VMEM)
    in_smem = pl.BlockSpec(memory_space=pltpu.SMEM)
    return pl.pallas_call(
        kernel,
        out_shape=(
            jax.ShapeDtypeStruct(eddy.shape, F32),
            jax.ShapeDtypeStruct(acoustic.shape, F32),
        ),
        in_specs=[anywhere, anywhere, anywhere, in_vmem, in_vmem, in_smem, in_smem],
        out_specs=(anywhere, anywhere),
        scratch_shapes=[
            vmem((5, 12, 2, FR, 128), F32),
            vmem((5, 10, 2, FR, 128), F32),
            vmem((5, 8, 2, 32, 128), F32),
            vmem((2048 + 16, 128), F32),
            vmem((128, 128, 128), jnp.bfloat16),
            vmem((512 + 16, 128), F32),
            vmem((DEV, 8, 128), F32),
            vmem((DEV + 1, 8, 128), F32),
            vmem((4, 4, 22, 2, AR, 128), F32),
            vmem((4, 2, 12, 16, 128), F32),
            vmem((4, 2, 12, 16, 128), F32),
            vmem((2, 20, 8, 128), F32),
            vmem((2, 20, 8, 128), F32),
            vmem((4, 16, 128), F32),
            vmem((4, 16, 128), F32),
            vmem((DEV, 2, 128), jnp.int32),
            vmem((2, DEV, 128), jnp.int32),
            vmem((2, DEV, 128), jnp.int32),
            vmem((2, 128), jnp.int32),
            pltpu.SMEM((2, 128), jnp.int32),
            vmem((512, 256), jnp.bfloat16),
            vmem((4, 512, 128), F32),
            vmem((4, 16, 2, 16, 128), F32),
            vmem((4, 16, 2, 16, 128), F32),
            dma((5,)), dma,
            dma((2,)), dma((2,)), dma((2,)), dma((2,)), dma((4,)), dma((4,)),
            dma, dma, dma, dma, dma, dma,
            dma((4, 2)), dma((4, 2)), dma((4, 2)), dma((4, 2)), dma((4,)),
        ],
        compiler_params=pltpu.CompilerParams(
            collective_id=0, has_side_effects=True, vmem_limit_bytes=52 * 1024 * 1024
        ),
        name="jet_step",
    )(
        eddy,
        acoustic,
        weights.reshape(128, 128, 128),
        target_device.reshape(1, 128),
        target_block.reshape(1, 128),
        source_block.reshape(128),
        live_count.reshape(1),
    )


def solution(mesh):
    placed = (
        P(None, "gx", "row", None),
        P(None, "gx", "row", None),
        P("gx", "row", None, None, None),
        P("gx", "row", None),
        P("gx", "row", None, None),
        P("gx", "row", None),
        P("gx", "row"),
    )
    return jax.shard_map(
        body,
        mesh=mesh,
        in_specs=placed,
        out_specs=(P(None, "gx", "row", None), P(None, "gx", "row", None)),
        check_vma=False,
    )
```

```python
import functools

import jax
import jax.numpy as jnp
from jax import lax
from jax.experimental import pallas as pl
from jax.experimental.pallas import tpu as pltpu
from jax.sharding import PartitionSpec as P

MESH = pl.DeviceIdType.MESH
F32 = jnp.float32

gamma_gas = 1.4
sound_timestep = 0.5
mean_mach = 0.3
stencil = (0.75, -0.15, 1.0 / 60.0)

GX = 8
ROW = 16
DEV = GX * ROW
FR = 48
AR = 32
CORNERS = ((0, 0), (0, 1), (1, 0), (1, 1))
RADIAL = (0, 2)


def shifted(low, high, lane, step):
    if step > 0:
        a, b = pltpu.roll(low, 128 - step, 1), pltpu.roll(high, 128 - step, 1)
        keep = lane < 128 - step
    else:
        a, b = pltpu.roll(low, -step, 1), pltpu.roll(high, -step, 1)
        keep = lane >= -step
    return jnp.where(keep, a, b), jnp.where(keep, b, a)


def flow_tile(src, x, row, lane, emit):
    rows = pl.ds(row, 8)
    center = [[src[c, x, zh, rows, :] for zh in range(2)] for c in range(5)]
    upper = [shifted(center[c][0], center[c][1], lane, 1) for c in range(5)]
    lower = [shifted(center[c][0], center[c][1], lane, -1) for c in range(5)]
    for zh in range(2):
        dx, dr, dz, lap = [], [], [], []
        for c in range(5):
            xp, xm = src[c, x + 1, zh, rows, :], src[c, x - 1, zh, rows, :]
            rp, rm = src[c, x, zh, pl.ds(row + 1, 8), :], src[c, x, zh, pl.ds(row - 1, 8), :]
            zp, zm = upper[c][zh], lower[c][zh]
            dx.append(xp - xm)
            dr.append(rp - rm)
            dz.append(zp - zm)
            lap.append(((xp + xm) + (rp + rm)) + ((zp + zm) - 6.0 * center[c][zh]))
        q = [center[c][zh] for c in range(5)]
        div = dx[1] + dr[2] + dz[3]
        rho = 1.0 + q[0]
        inv = 1.0 / rho
        force = (
            rho * div,
            dx[4] * inv,
            dr[4] * inv,
            dz[4] * inv,
            (gamma_gas * q[4] + 1.0) * div,
        )
        new = []
        for c in range(5):
            adv = q[1] * dx[c] + q[2] * dr[c] + q[3] * dz[c]
            new.append(q[c] + 0.1 * (lap[c] - adv - force[c]))
        emit(zh, new)


def rate_tile(src, x, row, lane):
    rows = pl.ds(row, 8)

    def grad_x(c, zh):
        total = None
        for k in range(3):
            part = stencil[k] * (src[c, x + 4 + k, zh, rows, :] - src[c, x + 2 - k, zh, rows, :])
            total = part if total is None else total + part
        return total

    def grad_r(c, zh):
        total = None
        for k in range(3):
            part = stencil[k] * (
                src[c, x + 3, zh, pl.ds(row + k + 1, 8), :]
                - src[c, x + 3, zh, pl.ds(row - k - 1, 8), :]
            )
            total = part if total is None else total + part
        return total

    def grad_z(c):
        low, high = src[c, x + 3, 0, rows, :], src[c, x + 3, 1, rows, :]
        total = None
        for k in range(3):
            up = shifted(low, high, lane, k + 1)
            down = shifted(low, high, lane, -k - 1)
            part = [stencil[k] * (up[zh] - down[zh]) for zh in range(2)]
            total = part if total is None else [total[zh] + part[zh] for zh in range(2)]
        return total

    zp, zw = grad_z(0), grad_z(3)
    out = []
    for zh in range(2):
        xp, xu, xv, xw = (grad_x(c, zh) for c in range(4))
        out.append(
            (
                -(mean_mach * xp + xu + grad_r(2, zh) + zw[zh]),
                -(mean_mach * xu + xp),
                -(mean_mach * xv + grad_r(0, zh)),
                -(mean_mach * xw + zp[zh]),
            )
        )
    return out


def kernel(
    eddy, acoustic, weights, numbers, eddy_out, final,
    f0, f1, f2, srcs, wv, contrib, outgoing, incoming, ys, rsend, rrecv, xrecv, fsend, frecv, csend, crecv,
    numbers_s, lists, square, turned, slots, slots_s, onehot, source,
    load_sem, small_sem, slot_sem, fx_s, fx_r, fr_s, fr_r, fc_s, fc_r, l1_s, l1_r, l2_s, l2_r, aa_s, aa_r,
    ax_s, ax_r, ar_s, ar_r, plane_in, all_in, out_sem,
):
    g, r = lax.axis_index("gx"), lax.axis_index("row")
    me = g * ROW + r
    left, right = lax.rem(g + GX - 1, GX), lax.rem(g + 1, GX)
    below, above = lax.rem(r + ROW - 1, ROW), lax.rem(r + 1, ROW)
    ry, rz = lax.div(r, 4), lax.rem(r, 4)
    lane = lax.broadcasted_iota(jnp.int32, (8, 128), 1)
    sub = lax.broadcasted_iota(jnp.int32, (8, 128), 0)
    zero = jnp.zeros((8, 128), F32)

    def remote(src, dst, send, recv, where):
        return pltpu.make_async_remote_copy(
            src_ref=src, dst_ref=dst, send_sem=send, recv_sem=recv, device_id=where, device_id_type=MESH
        )

    def signal(sem, where):
        pl.semaphore_signal(sem, inc=1, device_id=where, device_id_type=MESH)

    def y_line(k):
        return g, lax.rem(ry + k, 4) * 4 + rz

    def x_line(k):
        return lax.rem(g + k, GX), r

    small = pltpu.make_async_copy(numbers, numbers_s, small_sem)
    small.start()

    bar = pltpu.get_barrier_semaphore()
    for i, j in CORNERS:
        signal(bar, ((left, right)[i], (below, above)[j]))
    signal(bar, (g, below))
    signal(bar, (g, above))
    for k in range(1, 4):
        signal(bar, y_line(k))
        signal(bar, (g, ry * 4 + lax.rem(rz + k, 4)))
    for k in range(1, GX):
        signal(bar, x_line(k))

    loads = []
    for zh in range(2):
        lanes = pl.ds(128 * zh, 128)
        loads.append(
            pltpu.make_async_copy(
                eddy.at[:, :, :, lanes], f0.at[:, pl.ds(2, 8), zh, pl.ds(8, 32), :], load_sem.at[zh]
            )
        )
    for zh in range(2):
        lanes = pl.ds(128 * zh, 128)
        loads.append(
            pltpu.make_async_copy(
                acoustic.at[:, :, :, lanes],
                ys.at[0, :, pl.ds(3, 16), zh, pl.ds(8, 16), :],
                load_sem.at[2 + zh],
            )
        )
    loads.append(pltpu.make_async_copy(weights, wv, load_sem.at[4]))
    for copy in loads:
        copy.start()

    @pl.loop(0, 4)
    def _(n):
        @pl.loop(0, 3)
        def _(x):
            for c in range(4):
                for zh in range(2):
                    for line in (x, x + 19):
                        for t in (8, 16):
                            ys[n, c, line, zh, t : t + 8, :] = zero

        @pl.loop(3, 19)
        def _(x):
            for c in RADIAL:
                for zh in range(2):
                    for t in (0, 24):
                        ys[n, c, x, zh, t : t + 8, :] = zero

    @pl.when(r == 0)
    def _():
        f0[:, :, :, 0:8, :] = jnp.zeros((5, 12, 2, 8, 128), F32)

    @pl.when(r == ROW - 1)
    def _():
        f0[:, :, :, 40:48, :] = jnp.zeros((5, 12, 2, 8, 128), F32)

    entry = lax.broadcasted_iota(jnp.int32, (128, 128), 0)
    device = lax.broadcasted_iota(jnp.int32, (128, 128), 1)
    named = jnp.broadcast_to(numbers[0:1, :], (128, 128)).T
    block = jnp.broadcast_to(numbers[1:2, :], (128, 128)).T
    hit = (named == device) & (entry < numbers[3:4, :])
    first = jnp.min(jnp.where(hit, entry, 128), axis=0, keepdims=True)
    last = jnp.max(jnp.where(hit, entry, -1), axis=0, keepdims=True)
    id_first = jnp.max(jnp.where(hit & (entry == first), block, -1), axis=0, keepdims=True)
    id_last = jnp.max(jnp.where(hit & (entry == last), block, -1), axis=0, keepdims=True)
    slots[0:1, :] = jnp.where(first < 128, first, 0)
    slots[1:2, :] = jnp.maximum(last, 0)
    lists[me, 0:1, :] = id_first
    lists[me, 1:2, :] = jnp.where(last > first, id_last, -1)
    slot_copy = pltpu.make_async_copy(slots, slots_s, slot_sem)
    slot_copy.start()

    loads[0].wait()
    loads[1].wait()

    flat0 = f0.reshape(5 * 12 * 2 * FR, 128)

    def flow_row(c, x, zh, row):
        return ((c * 12 + x) * 2 + zh) * FR + row

    for side in range(2):
        for c in range(5):
            for k in range(2):
                for zh in range(2):
                    start = flow_row(c, 2, zh, (8, 38)[side] + k)
                    fsend[side, (c * 2 + k) * 2 + zh] = flat0[pl.ds(start, 8, stride=2 * FR), :]
    for n, (i, j) in enumerate(CORNERS):
        for c in range(5):
            for zh in range(2):
                start = flow_row(c, (2, 9)[i], zh, (8, 39)[j])
                csend[n, 2 * c + zh : 2 * c + zh + 1, :] = flat0[pl.ds(start, 1), :]

    inner = pl.ds(8, 32)
    flow_copies = [
        remote(fsend.at[0], frecv.at[0], fr_s.at[0], fr_r.at[0], (g, below)),
        remote(fsend.at[1], frecv.at[1], fr_s.at[1], fr_r.at[1], (g, above)),
        remote(
            f0.at[:, pl.ds(2, 2), :, inner, :], f0.at[:, pl.ds(10, 2), :, inner, :],
            fx_s.at[0], fx_r.at[0], (left, r),
        ),
        remote(
            f0.at[:, pl.ds(8, 2), :, inner, :], f0.at[:, pl.ds(0, 2), :, inner, :],
            fx_s.at[1], fx_r.at[1], (right, r),
        ),
    ]
    for n, (i, j) in enumerate(CORNERS):
        where = ((left, right)[i], (below, above)[j])
        flow_copies.append(remote(csend.at[n], crecv.at[n], fc_s.at[n], fc_r.at[n], where))

    pl.semaphore_wait(bar, 4 + 2 + 6 + GX - 1)
    for copy in flow_copies:
        copy.start()
    for k in range(1, 4):
        signal(plane_in, y_line(k))

    def first_step(x, tiles):
        for t in tiles:
            row = 7 + 8 * t

            def emit(zh, new):
                for c in range(5):
                    f1[c, x - 1, zh, pl.ds(row, 8), :] = new[c]

            flow_tile(f0, x, row, lane, emit)

    @pl.loop(3, 9, unroll=2)
    def _(x):
        first_step(x, (1, 2, 3))

    pl.semaphore_wait(plane_in, 3)
    for k in range(1, GX):
        signal(all_in, x_line(k))

    @pl.loop(1, ROW)
    def _(k):
        remote(lists.at[me], lists.at[me], l1_s, l1_r, (g, lax.rem(r + k, ROW))).start()

    flow_copies[0].wait_recv()
    flow_copies[1].wait_recv()

    def unpack_flow(side):
        for c in range(5):
            for k in range(2):
                for zh in range(2):
                    start = flow_row(c, 2, zh, (40, 6)[side] + k)
                    flat0[pl.ds(start, 8, stride=2 * FR), :] = frecv[side, (c * 2 + k) * 2 + zh]

    @pl.when(r < ROW - 1)
    def _():
        unpack_flow(0)

    @pl.when(r > 0)
    def _():
        unpack_flow(1)

    @pl.loop(3, 9, unroll=2)
    def _(x):
        first_step(x, (0, 4))

    for copy in flow_copies[2:]:
        copy.wait_recv()

    flats = ys.reshape(4 * 4 * 22 * 2 * AR, 128)
    points = pl.ds(8, 16)

    def acoustic_row(n, c, x, zh, row):
        return (((n * 4 + c) * 22 + x) * 2 + zh) * AR + row

    def acoustic_pack(n):
        for side in range(2):
            for m, c in enumerate(RADIAL):
                for k in range(3):
                    for zh in range(2):
                        for half in range(2):
                            start = acoustic_row(n, c, 3 + 8 * half, zh, (8, 21)[side] + k)
                            rsend[n, side, (m * 3 + k) * 2 + zh, 8 * half : 8 * half + 8, :] = flats[
                                pl.ds(start, 8, stride=2 * AR), :
                            ]

    def acoustic_send(n):
        copies = [
            remote(rsend.at[n, 0], rrecv.at[n, 0], ar_s.at[n, 0], ar_r.at[n, 0], (g, below)),
            remote(rsend.at[n, 1], rrecv.at[n, 1], ar_s.at[n, 1], ar_r.at[n, 1], (g, above)),
            remote(
                ys.at[n, :, pl.ds(3, 3), :, points, :], xrecv.at[n, 0],
                ax_s.at[n, 0], ax_r.at[n, 0], (left, r),
            ),
            remote(
                ys.at[n, :, pl.ds(16, 3), :, points, :], xrecv.at[n, 1],
                ax_s.at[n, 1], ax_r.at[n, 1], (right, r),
            ),
        ]
        for copy in copies:
            copy.start()
        return copies

    loads[2].wait()
    loads[3].wait()
    acoustic_pack(0)
    sent = [acoustic_send(0)]

    for n, (i, j) in enumerate(CORNERS):

        @pl.when(jnp.logical_and((g < GX - 1, g > 0)[i], (r < ROW - 1, r > 0)[j]))
        def _():
            for c in range(5):
                for zh in range(2):
                    start = flow_row(c, (10, 1)[i], zh, (40, 7)[j])
                    flat0[pl.ds(start, 1), :] = crecv[n, 2 * c + zh : 2 * c + zh + 1, :]

    @pl.when(g == 0)
    def _():
        f0[:, 0:2, :, :, :] = jnp.zeros((5, 2, 2, FR, 128), F32)

    @pl.when(g == GX - 1)
    def _():
        f0[:, 10:12, :, :, :] = jnp.zeros((5, 2, 2, FR, 128), F32)

    @pl.loop(0, 4, unroll=2)
    def _(n):
        first_step(n + 1 + 6 * lax.div(n, 2), range(5))

    @pl.when(g == 0)
    def _():
        f1[:, 0, :, :, :] = jnp.zeros((5, 2, FR, 128), F32)

    @pl.when(g == GX - 1)
    def _():
        f1[:, 9, :, :, :] = jnp.zeros((5, 2, FR, 128), F32)

    @pl.when(r == 0)
    def _():
        f1[:, :, :, 7:8, :] = jnp.zeros((5, 10, 2, 1, 128), F32)

    @pl.when(r == ROW - 1)
    def _():
        f1[:, :, :, 40:41, :] = jnp.zeros((5, 10, 2, 1, 128), F32)

    @pl.loop(0, 8, unroll=2)
    def _(x):
        for t in range(4):

            def emit(zh, new):
                for c in range(5):
                    f2[c, x, 8 * t : 8 * t + 8, 128 * zh : 128 * zh + 128] = new[c]
                rho = 1.0 + new[0]
                for c, value in enumerate((new[4], rho * new[1], rho * new[2], rho * new[3])):
                    srcs[pl.ds(8 + x * 256 + 64 * t + 4 * zh + c, 8, stride=8), :] = value

            flow_tile(f1, x + 1, 8 + 8 * t, lane, emit)

    flow_out = pltpu.make_async_copy(f2, eddy_out, out_sem)
    flow_out.start()
    pltpu.make_async_copy(lists.at[pl.ds(0, ROW - 1)], lists.at[pl.ds(0, ROW - 1)], l1_r).wait()
    pl.semaphore_wait(all_in, GX - 1)
    plane = lists.at[pl.ds(g * ROW, ROW)]

    @pl.loop(1, GX)
    def _(k):
        remote(plane, plane, l2_s, l2_r, x_line(k)).start()

    loads[4].wait()
    small.wait()

    @pl.loop(0, 8)
    def _(m):
        for u in range(8):
            p = m * 8 + u
            low = srcs[pl.ds(8 + 4 * numbers_s[2, 2 * p], 8), :]
            high = srcs[pl.ds(4 + 4 * numbers_s[2, 2 * p + 1], 8), :]
            lhs = jnp.concatenate(
                [jnp.where(sub < 4, low, 0.0), jnp.where(sub < 4, 0.0, high)], axis=1
            ).astype(jnp.bfloat16)
            rhs = jnp.concatenate([wv[2 * p], wv[2 * p + 1]], axis=1)
            contrib[pl.ds(8 + 8 * p, 8), :] = lax.dot_general(
                lhs, rhs, (((1,), (1,)), ((), ())), preferred_element_type=F32
            )

    slot_copy.wait()

    def slot_tile(d):
        low = contrib[pl.ds(8 + 4 * jnp.clip(slots_s[0, d], 0, 127), 8), :]
        high = contrib[pl.ds(4 + 4 * jnp.clip(slots_s[1, d], 0, 127), 8), :]
        return jnp.where(sub < 4, low, high)

    @pl.loop(1, DEV)
    def _(k):
        d = lax.rem(me + k, DEV)
        outgoing[d] = slot_tile(d)
        where = (lax.div(d, ROW), lax.rem(d, ROW))
        remote(outgoing.at[d], incoming.at[me], aa_s, aa_r, where).start()

    incoming[me] = slot_tile(me)

    def source_tile(c, x, zh, t):
        return source[c, pl.ds(pl.multiple_of(x * 32 + zh * 16 + 8 * t, 8), 8), :]

    def stage_bulk(n, step):
        @pl.loop(0, 16, unroll=4)
        def _(x):
            for t in range(2):
                rate = rate_tile(ys.at[n], x, 8 + 8 * t, lane)
                for zh in range(2):
                    for c in range(4):
                        old = ys[0, c, x + 3, zh, 8 + 8 * t : 16 + 8 * t, :]
                        change = rate[zh][c]
                        if n > 0:
                            change = change + source_tile(c, x, zh, t)
                        new = old + step * change
                        if n < 3:
                            ys[n + 1, c, x + 3, zh, 8 + 8 * t : 16 + 8 * t, :] = new
                        else:
                            final[c, x, 8 * t : 8 * t + 8, 128 * zh : 128 * zh + 128] = new

    def halo_share(lines, ell, upper):
        total = None
        for k in range(ell + 1, 4):
            part = stencil[k - 1] * (lines[k - ell - 1] if upper else lines[ell - k + 3])
            total = part if total is None else total + part
        return total if upper else -total

    def fix_x(n, step, side):
        for zh in range(2):
            for t in range(2):
                rows = pl.ds(8 * t, 8)
                halo = [[xrecv[n, side, c, k, zh, rows, :] for k in range(3)] for c in range(4)]
                for ell in range(3):
                    x = ell if side else 15 - ell
                    gp, gu, gv, gw = (halo_share(halo[c], ell, side == 0) for c in range(4))
                    changes = (mean_mach * gp + gu, mean_mach * gu + gp, mean_mach * gv, mean_mach * gw)
                    for c in range(4):
                        if n < 3:
                            at = (n + 1, c, x + 3, zh, pl.ds(8 + 8 * t, 8), slice(None))
                            ys[at] = ys[at] - step * changes[c]
                        else:
                            at = (c, x, rows, pl.ds(128 * zh, 128))
                            final[at] = final[at] - step * changes[c]

    def clear_ends(n):
        @pl.when(r == ROW - 1)
        def _():
            rrecv[n, 0] = jnp.zeros((12, 16, 128), F32)

        @pl.when(r == 0)
        def _():
            rrecv[n, 1] = jnp.zeros((12, 16, 128), F32)

    def fix_r(n, step):
        for side in range(2):
            for zh in range(2):
                for half in range(2):
                    eight = pl.ds(8 * half, 8)
                    halo = [
                        [rrecv[n, side, (m * 3 + k) * 2 + zh, eight, :] for k in range(3)] for m in range(2)
                    ]
                    for ell in range(3):
                        row = ell if side else 15 - ell
                        for m, c in enumerate(RADIAL):
                            change = step * halo_share(halo[1 - m], ell, side == 0)
                            start = acoustic_row(n + 1, c, 3 + 8 * half, zh, 8 + row)
                            at = pl.ds(start, 8, stride=2 * AR)
                            new = flats[at, :] - change
                            flats[at, :] = new
                            if n > 0:
                                k = ell if side else 2 - ell
                                rsend[n + 1, 1 - side, (m * 3 + k) * 2 + zh, eight, :] = new

    def fix_r_last(n, step):
        for side in range(2):
            for m, c in enumerate(RADIAL):
                for k in range(3):
                    for zh in range(2):
                        for half in range(2):
                            start = acoustic_row(n, c, 3 + 8 * half, zh, (24, 5)[side] + k)
                            flats[pl.ds(start, 8, stride=2 * AR), :] = rrecv[
                                n, side, (m * 3 + k) * 2 + zh, 8 * half : 8 * half + 8, :
                            ]

        @pl.loop(0, 16, unroll=4)
        def _(x):
            for side in range(2):
                for zh in range(2):
                    for m, c in enumerate(RADIAL):
                        other = RADIAL[1 - m]
                        total = None
                        for k in range(1, 4):
                            if side:
                                part = jnp.where(sub < k, ys[n, other, x + 3, zh, pl.ds(8 - k, 8), :], 0.0)
                                part = (-step * stencil[k - 1]) * part
                            else:
                                part = jnp.where(sub >= 8 - k, ys[n, other, x + 3, zh, pl.ds(16 + k, 8), :], 0.0)
                                part = (step * stencil[k - 1]) * part
                            total = part if total is None else total + part
                        at = (c, x, pl.ds(0 if side else 8, 8), pl.ds(128 * zh, 128))
                        final[at] = final[at] - total

    def stage_fix(n, step):
        sent[n][2].wait_recv()
        sent[n][3].wait_recv()

        @pl.when(g < GX - 1)
        def _():
            fix_x(n, step, 0)

        @pl.when(g > 0)
        def _():
            fix_x(n, step, 1)

        sent[n][0].wait_recv()
        sent[n][1].wait_recv()
        clear_ends(n)
        if n < 3:
            fix_r(n, step)
        else:
            fix_r_last(n, step)

    stage_bulk(0, sound_timestep / 4.0)
    stage_fix(0, sound_timestep / 4.0)

    rest = pl.ds(0, DEV - ROW)
    pltpu.make_async_copy(lists.at[rest], lists.at[rest], l2_r).wait()

    @pl.loop(0, DEV, unroll=8)
    def _(j):
        for k in range(2):
            square[k, pl.ds(j, 1), :] = lists[j, k : k + 1, :]

    for k in range(2):
        turned[k] = square[k].T
    ids = [turned[k, pl.ds(me, 1), :] for k in range(2)]

    @pl.loop(0, 16)
    def _(x):
        place = lax.broadcasted_iota(jnp.int32, (32, 128), 0)
        place = (x * 16 + lax.rem(place, 16)) * 2 + lax.div(place, 16)
        for k in range(2):
            onehot[pl.ds(pl.multiple_of(x * 32, 32), 32), 128 * k : 128 * k + 128] = jnp.where(
                place == ids[k], 1.0, 0.0
            ).astype(jnp.bfloat16)

    others = pl.ds(0, DEV - 1)
    pltpu.make_async_copy(incoming.at[others], incoming.at[others], aa_r).wait()

    flat_in = incoming.reshape((DEV + 1) * 8, 128)
    for pair in range(2):
        value = jnp.concatenate(
            [
                jnp.concatenate(
                    [flat_in[pl.ds(4 * k + 2 * pair + c, DEV, stride=8), :] for k in range(2)], axis=0
                )
                for c in range(2)
            ],
            axis=1,
        )
        high = value.astype(jnp.bfloat16)
        low = (value - high.astype(F32)).astype(jnp.bfloat16)

        @pl.loop(0, 4)
        def _(q):
            rows = onehot[pl.ds(pl.multiple_of(q * 128, 128), 128), :]
            total = jnp.dot(rows, high, preferred_element_type=F32) + jnp.dot(
                rows, low, preferred_element_type=F32
            )
            for c in range(2):
                part = total[:, 128 * c : 128 * c + 128]
                source[2 * pair + c, pl.ds(pl.multiple_of(q * 128, 128), 128), :] = part
                for i in range(4):
                    for zh in range(2):
                        at = (1, 2 * pair + c, q * 4 + i + 3, zh, points, slice(None))
                        piece = part[32 * i + 16 * zh : 32 * i + 16 * zh + 16, :]
                        ys[at] = ys[at] + (sound_timestep / 4.0) * piece

    acoustic_pack(1)
    for n in range(1, 4):
        sent.append(acoustic_send(n))
        stage_bulk(n, sound_timestep / (4 - n))
        stage_fix(n, sound_timestep / (4 - n))

    for copy in flow_copies:
        copy.wait_send()
    for copies in sent:
        for copy in copies:
            copy.wait_send()
    pltpu.make_async_copy(lists.at[pl.ds(0, ROW - 1)], lists.at[pl.ds(0, ROW - 1)], l1_s).wait()
    pltpu.make_async_copy(lists.at[rest], lists.at[rest], l2_s).wait()
    pltpu.make_async_copy(outgoing.at[others], outgoing.at[others], aa_s).wait()
    flow_out.wait()


def body(eddy, acoustic, weights, source_block, target_device, target_block, live_count):
    vmem, dma, regular = pltpu.VMEM, pltpu.SemaphoreType.DMA, pltpu.SemaphoreType.REGULAR
    anywhere = pl.BlockSpec(memory_space=pl.ANY)
    in_vmem = pl.BlockSpec(memory_space=pltpu.VMEM)
    numbers = jnp.concatenate(
        [
            target_device.reshape(1, 128),
            target_block.reshape(1, 128),
            source_block.reshape(1, 128),
            jnp.broadcast_to(live_count, (1, 128)),
        ]
    )
    return pl.pallas_call(
        kernel,
        out_shape=(
            jax.ShapeDtypeStruct(eddy.shape, F32),
            jax.ShapeDtypeStruct(acoustic.shape, F32),
        ),
        in_specs=[anywhere] * 3 + [in_vmem],
        out_specs=(anywhere, in_vmem),
        scratch_shapes=[
            vmem((5, 12, 2, FR, 128), F32),
            vmem((5, 10, 2, FR, 128), F32),
            vmem((5, 8, 32, 256), F32),
            vmem((2048 + 16, 128), F32),
            vmem((128, 128, 128), jnp.bfloat16),
            vmem((512 + 16, 128), F32),
            vmem((DEV, 8, 128), F32),
            vmem((DEV + 1, 8, 128), F32),
            vmem((4, 4, 22, 2, AR, 128), F32),
            vmem((4, 2, 12, 16, 128), F32),
            vmem((4, 2, 12, 16, 128), F32),
            vmem((4, 2, 4, 3, 2, 16, 128), F32),
            vmem((2, 20, 8, 128), F32),
            vmem((2, 20, 8, 128), F32),
            vmem((4, 16, 128), F32),
            vmem((4, 16, 128), F32),
            pltpu.SMEM((4, 128), jnp.int32),
            vmem((DEV, 2, 128), jnp.int32),
            vmem((2, DEV, 128), jnp.int32),
            vmem((2, DEV, 128), jnp.int32),
            vmem((2, 128), jnp.int32),
            pltpu.SMEM((2, 128), jnp.int32),
            vmem((512, 256), jnp.bfloat16),
            vmem((4, 512, 128), F32),
            dma((5,)), dma, dma,
            dma((2,)), dma((2,)), dma((2,)), dma((2,)), dma((4,)), dma((4,)),
            dma, dma, dma, dma, dma, dma,
            dma((4, 2)), dma((4, 2)), dma((4, 2)), dma((4, 2)), regular, regular, dma,
        ],
        compiler_params=pltpu.CompilerParams(
            collective_id=0, has_side_effects=True, vmem_limit_bytes=52 * 1024 * 1024
        ),
        name="jet_step",
    )(
        eddy,
        acoustic,
        weights.reshape(128, 128, 128),
        numbers,
    )


def solution(mesh):
    placed = (
        P(None, "gx", "row", None),
        P(None, "gx", "row", None),
        P("gx", "row", None, None, None),
        P("gx", "row", None),
        P("gx", "row", None, None),
        P("gx", "row", None),
        P("gx", "row"),
    )
    return jax.shard_map(
        body,
        mesh=mesh,
        in_specs=placed,
        out_specs=(P(None, "gx", "row", None), P(None, "gx", "row", None)),
        check_vma=False,
    )
```

```python
import functools

import jax
import jax.numpy as jnp
from jax import lax
from jax.experimental import pallas as pl
from jax.experimental.pallas import tpu as pltpu
from jax.sharding import PartitionSpec as P

MESH = pl.DeviceIdType.MESH
F32 = jnp.float32

gamma_gas = 1.4
sound_timestep = 0.5
mean_mach = 0.3
stencil = (0.75, -0.15, 1.0 / 60.0)

GX = 8
ROW = 16
DEV = GX * ROW
FR = 48
AR = 32
CORNERS = ((0, 0), (0, 1), (1, 0), (1, 1))
RADIAL = (0, 2)


def shifted(low, high, lane, step):
    if step > 0:
        a, b = pltpu.roll(low, 128 - step, 1), pltpu.roll(high, 128 - step, 1)
        keep = lane < 128 - step
    else:
        a, b = pltpu.roll(low, -step, 1), pltpu.roll(high, -step, 1)
        keep = lane >= -step
    return jnp.where(keep, a, b), jnp.where(keep, b, a)


def flow_tile(src, x, row, lane, emit):
    rows = pl.ds(row, 8)
    center = [[src[c, x, zh, rows, :] for zh in range(2)] for c in range(5)]
    upper = [shifted(center[c][0], center[c][1], lane, 1) for c in range(5)]
    lower = [shifted(center[c][0], center[c][1], lane, -1) for c in range(5)]
    for zh in range(2):
        dx, dr, dz, lap = [], [], [], []
        for c in range(5):
            xp, xm = src[c, x + 1, zh, rows, :], src[c, x - 1, zh, rows, :]
            rp, rm = src[c, x, zh, pl.ds(row + 1, 8), :], src[c, x, zh, pl.ds(row - 1, 8), :]
            zp, zm = upper[c][zh], lower[c][zh]
            dx.append(xp - xm)
            dr.append(rp - rm)
            dz.append(zp - zm)
            lap.append(((xp + xm) + (rp + rm)) + ((zp + zm) - 6.0 * center[c][zh]))
        q = [center[c][zh] for c in range(5)]
        div = dx[1] + dr[2] + dz[3]
        rho = 1.0 + q[0]
        inv = 1.0 / rho
        force = (
            rho * div,
            dx[4] * inv,
            dr[4] * inv,
            dz[4] * inv,
            (gamma_gas * q[4] + 1.0) * div,
        )
        new = []
        for c in range(5):
            adv = q[1] * dx[c] + q[2] * dr[c] + q[3] * dz[c]
            new.append(q[c] + 0.1 * (lap[c] - adv - force[c]))
        emit(zh, new)


def rate_tile(src, x, row, lane):
    rows = pl.ds(row, 8)

    def grad_x(c, zh):
        total = None
        for k in range(3):
            part = stencil[k] * (src[c, x + 4 + k, zh, rows, :] - src[c, x + 2 - k, zh, rows, :])
            total = part if total is None else total + part
        return total

    def grad_r(c, zh):
        total = None
        for k in range(3):
            part = stencil[k] * (
                src[c, x + 3, zh, pl.ds(row + k + 1, 8), :]
                - src[c, x + 3, zh, pl.ds(row - k - 1, 8), :]
            )
            total = part if total is None else total + part
        return total

    def grad_z(c):
        low, high = src[c, x + 3, 0, rows, :], src[c, x + 3, 1, rows, :]
        total = None
        for k in range(3):
            up = shifted(low, high, lane, k + 1)
            down = shifted(low, high, lane, -k - 1)
            part = [stencil[k] * (up[zh] - down[zh]) for zh in range(2)]
            total = part if total is None else [total[zh] + part[zh] for zh in range(2)]
        return total

    zp, zw = grad_z(0), grad_z(3)
    out = []
    for zh in range(2):
        xp, xu, xv, xw = (grad_x(c, zh) for c in range(4))
        out.append(
            (
                -(mean_mach * xp + xu + grad_r(2, zh) + zw[zh]),
                -(mean_mach * xu + xp),
                -(mean_mach * xv + grad_r(0, zh)),
                -(mean_mach * xw + zp[zh]),
            )
        )
    return out


def kernel(
    eddy, acoustic, weights, numbers, eddy_out, final,
    f0, f1, f2, srcs, wv, contrib, outgoing, incoming, ys, rsend, rrecv, xrecv, fsend, frecv, csend, crecv,
    numbers_s, lists, square, turned, slots, slots_s, onehot, source,
    load_sem, small_sem, slot_sem, fx_s, fx_r, fr_s, fr_r, fc_s, fc_r, l1_s, l1_r, l2_s, l2_r, aa_s, aa_r,
    ax_s, ax_r, ar_s, ar_r, plane_in, all_in, out_sem,
):
    g, r = lax.axis_index("gx"), lax.axis_index("row")
    me = g * ROW + r
    left, right = lax.rem(g + GX - 1, GX), lax.rem(g + 1, GX)
    below, above = lax.rem(r + ROW - 1, ROW), lax.rem(r + 1, ROW)
    ry, rz = lax.div(r, 4), lax.rem(r, 4)
    lane = lax.broadcasted_iota(jnp.int32, (8, 128), 1)
    sub = lax.broadcasted_iota(jnp.int32, (8, 128), 0)
    zero = jnp.zeros((8, 128), F32)

    def remote(src, dst, send, recv, where):
        return pltpu.make_async_remote_copy(
            src_ref=src, dst_ref=dst, send_sem=send, recv_sem=recv, device_id=where, device_id_type=MESH
        )

    def signal(sem, where):
        pl.semaphore_signal(sem, inc=1, device_id=where, device_id_type=MESH)

    def y_line(k):
        return g, lax.rem(ry + k, 4) * 4 + rz

    def x_line(k):
        return lax.rem(g + k, GX), r

    bar = pltpu.get_barrier_semaphore()
    for i, j in CORNERS:
        signal(bar, ((left, right)[i], (below, above)[j]))
    signal(bar, (g, below))
    signal(bar, (g, above))
    for k in range(1, 4):
        signal(bar, y_line(k))
        signal(bar, (g, ry * 4 + lax.rem(rz + k, 4)))
    for k in range(1, GX):
        signal(bar, x_line(k))

    loads = []
    for zh in range(2):
        lanes = pl.ds(128 * zh, 128)
        loads.append(
            pltpu.make_async_copy(
                eddy.at[:, :, :, lanes], f0.at[:, pl.ds(2, 8), zh, pl.ds(8, 32), :], load_sem.at[zh]
            )
        )
    for zh in range(2):
        lanes = pl.ds(128 * zh, 128)
        loads.append(
            pltpu.make_async_copy(
                acoustic.at[:, :, :, lanes],
                ys.at[0, :, pl.ds(3, 16), zh, pl.ds(8, 16), :],
                load_sem.at[2 + zh],
            )
        )
    loads.append(pltpu.make_async_copy(weights, wv, load_sem.at[4]))
    loads[0].start()
    loads[1].start()

    @pl.when(r == 0)
    def _():
        f0[:, :, :, 0:8, :] = jnp.zeros((5, 12, 2, 8, 128), F32)

    @pl.when(r == ROW - 1)
    def _():
        f0[:, :, :, 40:48, :] = jnp.zeros((5, 12, 2, 8, 128), F32)

    loads[0].wait()
    loads[1].wait()
    small = pltpu.make_async_copy(numbers, numbers_s, small_sem)
    small.start()
    for copy in loads[2:]:
        copy.start()

    flat0 = f0.reshape(5 * 12 * 2 * FR, 128)

    def flow_row(c, x, zh, row):
        return ((c * 12 + x) * 2 + zh) * FR + row

    for side in range(2):
        for c in range(5):
            for k in range(2):
                for zh in range(2):
                    start = flow_row(c, 2, zh, (8, 38)[side] + k)
                    fsend[side, (c * 2 + k) * 2 + zh] = flat0[pl.ds(start, 8, stride=2 * FR), :]
    for n, (i, j) in enumerate(CORNERS):
        for c in range(5):
            for zh in range(2):
                start = flow_row(c, (2, 9)[i], zh, (8, 39)[j])
                csend[n, 2 * c + zh : 2 * c + zh + 1, :] = flat0[pl.ds(start, 1), :]

    inner = pl.ds(8, 32)
    flow_copies = [
        remote(fsend.at[0], frecv.at[0], fr_s.at[0], fr_r.at[0], (g, below)),
        remote(fsend.at[1], frecv.at[1], fr_s.at[1], fr_r.at[1], (g, above)),
        remote(
            f0.at[:, pl.ds(2, 2), :, inner, :], f0.at[:, pl.ds(10, 2), :, inner, :],
            fx_s.at[0], fx_r.at[0], (left, r),
        ),
        remote(
            f0.at[:, pl.ds(8, 2), :, inner, :], f0.at[:, pl.ds(0, 2), :, inner, :],
            fx_s.at[1], fx_r.at[1], (right, r),
        ),
    ]
    for n, (i, j) in enumerate(CORNERS):
        where = ((left, right)[i], (below, above)[j])
        flow_copies.append(remote(csend.at[n], crecv.at[n], fc_s.at[n], fc_r.at[n], where))

    pl.semaphore_wait(bar, 4 + 2 + 6 + GX - 1)
    for copy in flow_copies[2:4] + flow_copies[:2] + flow_copies[4:]:
        copy.start()
    for k in range(1, 4):
        signal(plane_in, y_line(k))

    entry = lax.broadcasted_iota(jnp.int32, (128, 128), 0)
    device = lax.broadcasted_iota(jnp.int32, (128, 128), 1)
    named = jnp.broadcast_to(numbers[0:1, :], (128, 128)).T
    block = jnp.broadcast_to(numbers[1:2, :], (128, 128)).T
    hit = (named == device) & (entry < numbers[3:4, :])
    first = jnp.min(jnp.where(hit, entry, 128), axis=0, keepdims=True)
    last = jnp.max(jnp.where(hit, entry, -1), axis=0, keepdims=True)
    id_first = jnp.max(jnp.where(hit & (entry == first), block, -1), axis=0, keepdims=True)
    id_last = jnp.max(jnp.where(hit & (entry == last), block, -1), axis=0, keepdims=True)
    slots[0:1, :] = jnp.where(first < 128, first, 0)
    slots[1:2, :] = jnp.maximum(last, 0)
    lists[me, 0:1, :] = id_first
    lists[me, 1:2, :] = jnp.where(last > first, id_last, -1)
    slot_copy = pltpu.make_async_copy(slots, slots_s, slot_sem)
    slot_copy.start()

    @pl.loop(0, 4)
    def _(n):
        @pl.loop(0, 3)
        def _(x):
            for c in range(4):
                for zh in range(2):
                    for line in (x, x + 19):
                        for t in (8, 16):
                            ys[n, c, line, zh, t : t + 8, :] = zero

        @pl.loop(3, 19)
        def _(x):
            for c in RADIAL:
                for zh in range(2):
                    for t in (0, 24):
                        ys[n, c, x, zh, t : t + 8, :] = zero

    def clear_flow_rows(low, high):
        for row, end in ((7, r == 0), (40, r == ROW - 1)):

            @pl.when(end)
            def _():
                f1[:, low:high, :, row : row + 1, :] = jnp.zeros((5, high - low, 2, 1, 128), F32)

    def first_step(x, tiles):
        for t in tiles:
            row = 7 + 8 * t

            def emit(zh, new):
                for c in range(5):
                    f1[c, x - 1, zh, pl.ds(row, 8), :] = new[c]

            flow_tile(f0, x, row, lane, emit)

    @pl.loop(3, 9, unroll=2)
    def _(x):
        first_step(x, (1, 2, 3))

    pl.semaphore_wait(plane_in, 3)
    for k in range(1, GX):
        signal(all_in, x_line(k))

    @pl.loop(1, ROW)
    def _(k):
        remote(lists.at[me], lists.at[me], l1_s, l1_r, (g, lax.rem(r + k, ROW))).start()

    flow_copies[0].wait_recv()
    flow_copies[1].wait_recv()

    def unpack_flow(side):
        for c in range(5):
            for k in range(2):
                for zh in range(2):
                    start = flow_row(c, 2, zh, (40, 6)[side] + k)
                    flat0[pl.ds(start, 8, stride=2 * FR), :] = frecv[side, (c * 2 + k) * 2 + zh]

    @pl.when(r < ROW - 1)
    def _():
        unpack_flow(0)

    @pl.when(r > 0)
    def _():
        unpack_flow(1)

    @pl.loop(3, 9, unroll=2)
    def _(x):
        first_step(x, (0, 4))

    def second_step(x):
        for t in range(4):

            def emit(zh, new):
                for c in range(5):
                    f2[c, x, 8 * t : 8 * t + 8, 128 * zh : 128 * zh + 128] = new[c]
                rho = 1.0 + new[0]
                for c, value in enumerate((new[4], rho * new[1], rho * new[2], rho * new[3])):
                    srcs[pl.ds(8 + x * 256 + 64 * t + 4 * zh + c, 8, stride=8), :] = value

            flow_tile(f1, x + 1, 8 + 8 * t, lane, emit)

    clear_flow_rows(2, 8)

    @pl.loop(2, 6, unroll=2)
    def _(x):
        second_step(x)

    for copy in flow_copies[2:]:
        copy.wait_recv()

    flats = ys.reshape(4 * 4 * 22 * 2 * AR, 128)
    points = pl.ds(8, 16)

    def acoustic_row(n, c, x, zh, row):
        return (((n * 4 + c) * 22 + x) * 2 + zh) * AR + row

    def acoustic_pack(n):
        for side in range(2):
            for m, c in enumerate(RADIAL):
                for k in range(3):
                    for zh in range(2):
                        for half in range(2):
                            start = acoustic_row(n, c, 3 + 8 * half, zh, (8, 21)[side] + k)
                            rsend[n, side, (m * 3 + k) * 2 + zh, 8 * half : 8 * half + 8, :] = flats[
                                pl.ds(start, 8, stride=2 * AR), :
                            ]

    def acoustic_send(n):
        copies = [
            remote(rsend.at[n, 0], rrecv.at[n, 0], ar_s.at[n, 0], ar_r.at[n, 0], (g, below)),
            remote(rsend.at[n, 1], rrecv.at[n, 1], ar_s.at[n, 1], ar_r.at[n, 1], (g, above)),
            remote(
                ys.at[n, :, pl.ds(3, 3), :, points, :], xrecv.at[n, 0],
                ax_s.at[n, 0], ax_r.at[n, 0], (left, r),
            ),
            remote(
                ys.at[n, :, pl.ds(16, 3), :, points, :], xrecv.at[n, 1],
                ax_s.at[n, 1], ax_r.at[n, 1], (right, r),
            ),
        ]
        for copy in copies:
            copy.start()
        return copies

    loads[2].wait()
    loads[3].wait()
    acoustic_pack(0)
    sent = [acoustic_send(0)]

    for n, (i, j) in enumerate(CORNERS):

        @pl.when(jnp.logical_and((g < GX - 1, g > 0)[i], (r < ROW - 1, r > 0)[j]))
        def _():
            for c in range(5):
                for zh in range(2):
                    start = flow_row(c, (10, 1)[i], zh, (40, 7)[j])
                    flat0[pl.ds(start, 1), :] = crecv[n, 2 * c + zh : 2 * c + zh + 1, :]

    @pl.when(g == 0)
    def _():
        f0[:, 0:2, :, :, :] = jnp.zeros((5, 2, 2, FR, 128), F32)

    @pl.when(g == GX - 1)
    def _():
        f0[:, 10:12, :, :, :] = jnp.zeros((5, 2, 2, FR, 128), F32)

    @pl.loop(0, 4, unroll=2)
    def _(n):
        first_step(n + 1 + 6 * lax.div(n, 2), range(5))

    @pl.when(g == 0)
    def _():
        f1[:, 0, :, :, :] = jnp.zeros((5, 2, FR, 128), F32)

    @pl.when(g == GX - 1)
    def _():
        f1[:, 9, :, :, :] = jnp.zeros((5, 2, FR, 128), F32)

    clear_flow_rows(1, 2)
    clear_flow_rows(8, 9)

    @pl.loop(0, 4, unroll=2)
    def _(n):
        second_step(n + 4 * lax.div(n, 2))

    flow_out = pltpu.make_async_copy(f2, eddy_out, out_sem)
    flow_out.start()
    pltpu.make_async_copy(lists.at[pl.ds(0, ROW - 1)], lists.at[pl.ds(0, ROW - 1)], l1_r).wait()
    pl.semaphore_wait(all_in, GX - 1)
    plane = lists.at[pl.ds(g * ROW, ROW)]

    @pl.loop(1, GX)
    def _(k):
        remote(plane, plane, l2_s, l2_r, x_line(k)).start()

    loads[4].wait()
    small.wait()

    @pl.loop(0, 8, unroll=2)
    def _(m):
        for u in range(8):
            p = m * 8 + u
            low = srcs[pl.ds(8 + 4 * numbers_s[2, 2 * p], 8), :]
            high = srcs[pl.ds(4 + 4 * numbers_s[2, 2 * p + 1], 8), :]
            lhs = jnp.concatenate(
                [jnp.where(sub < 4, low, 0.0), jnp.where(sub < 4, 0.0, high)], axis=1
            ).astype(jnp.bfloat16)
            rhs = jnp.concatenate([wv[2 * p], wv[2 * p + 1]], axis=1)
            contrib[pl.ds(8 + 8 * p, 8), :] = lax.dot_general(
                lhs, rhs, (((1,), (1,)), ((), ())), preferred_element_type=F32
            )

    slot_copy.wait()

    def slot_tile(d):
        low = contrib[pl.ds(8 + 4 * jnp.clip(slots_s[0, d], 0, 127), 8), :]
        high = contrib[pl.ds(4 + 4 * jnp.clip(slots_s[1, d], 0, 127), 8), :]
        return jnp.where(sub < 4, low, high)

    @pl.loop(1, DEV, unroll=6)
    def _(k):
        d = lax.rem(me + k, DEV)
        outgoing[d] = slot_tile(d)
        where = (lax.div(d, ROW), lax.rem(d, ROW))
        remote(outgoing.at[d], incoming.at[me], aa_s, aa_r, where).start()

    incoming[me] = slot_tile(me)

    def source_tile(c, x, zh, t):
        return source[c, pl.ds(pl.multiple_of(x * 32 + zh * 16 + 8 * t, 8), 8), :]

    def stage_bulk(n, step):
        @pl.loop(0, 16, unroll=4)
        def _(x):
            for t in range(2):
                rate = rate_tile(ys.at[n], x, 8 + 8 * t, lane)
                for zh in range(2):
                    for c in range(4):
                        old = ys[0, c, x + 3, zh, 8 + 8 * t : 16 + 8 * t, :]
                        change = rate[zh][c]
                        if n > 0:
                            change = change + source_tile(c, x, zh, t)
                        new = old + step * change
                        if n < 3:
                            ys[n + 1, c, x + 3, zh, 8 + 8 * t : 16 + 8 * t, :] = new
                        else:
                            final[c, x, 8 * t : 8 * t + 8, 128 * zh : 128 * zh + 128] = new

    def halo_share(lines, ell, upper):
        total = None
        for k in range(ell + 1, 4):
            part = stencil[k - 1] * (lines[k - ell - 1] if upper else lines[ell - k + 3])
            total = part if total is None else total + part
        return total if upper else -total

    def fix_x(n, step, side):
        for zh in range(2):
            for t in range(2):
                rows = pl.ds(8 * t, 8)
                halo = [[xrecv[n, side, c, k, zh, rows, :] for k in range(3)] for c in range(4)]
                for ell in range(3):
                    x = ell if side else 15 - ell
                    gp, gu, gv, gw = (halo_share(halo[c], ell, side == 0) for c in range(4))
                    changes = (mean_mach * gp + gu, mean_mach * gu + gp, mean_mach * gv, mean_mach * gw)
                    for c in range(4):
                        if n < 3:
                            at = (n + 1, c, x + 3, zh, pl.ds(8 + 8 * t, 8), slice(None))
                            ys[at] = ys[at] - step * changes[c]
                        else:
                            at = (c, x, rows, pl.ds(128 * zh, 128))
                            final[at] = final[at] - step * changes[c]

    def clear_ends(n):
        @pl.when(r == ROW - 1)
        def _():
            rrecv[n, 0] = jnp.zeros((12, 16, 128), F32)

        @pl.when(r == 0)
        def _():
            rrecv[n, 1] = jnp.zeros((12, 16, 128), F32)

    def fix_r(n, step):
        for side in range(2):
            for zh in range(2):
                for half in range(2):
                    eight = pl.ds(8 * half, 8)
                    halo = [
                        [rrecv[n, side, (m * 3 + k) * 2 + zh, eight, :] for k in range(3)] for m in range(2)
                    ]
                    for ell in range(3):
                        row = ell if side else 15 - ell
                        for m, c in enumerate(RADIAL):
                            change = step * halo_share(halo[1 - m], ell, side == 0)
                            start = acoustic_row(n + 1, c, 3 + 8 * half, zh, 8 + row)
                            at = pl.ds(start, 8, stride=2 * AR)
                            new = flats[at, :] - change
                            flats[at, :] = new
                            if n > 0:
                                k = ell if side else 2 - ell
                                rsend[n + 1, 1 - side, (m * 3 + k) * 2 + zh, eight, :] = new

    def fix_r_last(n, step):
        for side in range(2):
            for m, c in enumerate(RADIAL):
                for k in range(3):
                    for zh in range(2):
                        for half in range(2):
                            start = acoustic_row(n, c, 3 + 8 * half, zh, (24, 5)[side] + k)
                            flats[pl.ds(start, 8, stride=2 * AR), :] = rrecv[
                                n, side, (m * 3 + k) * 2 + zh, 8 * half : 8 * half + 8, :
                            ]

        @pl.loop(0, 16, unroll=4)
        def _(x):
            for side in range(2):
                for zh in range(2):
                    for m, c in enumerate(RADIAL):
                        other = RADIAL[1 - m]
                        total = None
                        for k in range(1, 4):
                            if side:
                                part = jnp.where(sub < k, ys[n, other, x + 3, zh, pl.ds(8 - k, 8), :], 0.0)
                                part = (-step * stencil[k - 1]) * part
                            else:
                                part = jnp.where(sub >= 8 - k, ys[n, other, x + 3, zh, pl.ds(16 + k, 8), :], 0.0)
                                part = (step * stencil[k - 1]) * part
                            total = part if total is None else total + part
                        at = (c, x, pl.ds(0 if side else 8, 8), pl.ds(128 * zh, 128))
                        final[at] = final[at] - total

    def stage_fix(n, step):
        sent[n][2].wait_recv()
        sent[n][3].wait_recv()

        @pl.when(g < GX - 1)
        def _():
            fix_x(n, step, 0)

        @pl.when(g > 0)
        def _():
            fix_x(n, step, 1)

        sent[n][0].wait_recv()
        sent[n][1].wait_recv()
        clear_ends(n)
        if n < 3:
            fix_r(n, step)
        else:
            fix_r_last(n, step)

    stage_bulk(0, sound_timestep / 4.0)
    stage_fix(0, sound_timestep / 4.0)

    rest = pl.ds(0, DEV - ROW)
    pltpu.make_async_copy(lists.at[rest], lists.at[rest], l2_r).wait()

    @pl.loop(0, DEV, unroll=8)
    def _(j):
        for k in range(2):
            square[k, pl.ds(j, 1), :] = lists[j, k : k + 1, :]

    for k in range(2):
        turned[k] = square[k].T
    ids = [turned[k, pl.ds(me, 1), :] for k in range(2)]

    @pl.loop(0, 16)
    def _(x):
        place = lax.broadcasted_iota(jnp.int32, (32, 128), 0)
        place = (x * 16 + lax.rem(place, 16)) * 2 + lax.div(place, 16)
        for k in range(2):
            onehot[pl.ds(pl.multiple_of(x * 32, 32), 32), 128 * k : 128 * k + 128] = jnp.where(
                place == ids[k], 1.0, 0.0
            ).astype(jnp.bfloat16)

    others = pl.ds(0, DEV - 1)
    pltpu.make_async_copy(incoming.at[others], incoming.at[others], aa_r).wait()

    flat_in = incoming.reshape((DEV + 1) * 8, 128)
    for pair in range(2):
        value = jnp.concatenate(
            [
                jnp.concatenate(
                    [flat_in[pl.ds(4 * k + 2 * pair + c, DEV, stride=8), :] for k in range(2)], axis=0
                )
                for c in range(2)
            ],
            axis=1,
        )
        high = value.astype(jnp.bfloat16)
        low = (value - high.astype(F32)).astype(jnp.bfloat16)

        rows = onehot[...]
        total = jnp.dot(rows, high, preferred_element_type=F32) + jnp.dot(
            rows, low, preferred_element_type=F32
        )
        for c in range(2):
            part = total[:, 128 * c : 128 * c + 128]
            source[2 * pair + c] = part
            for x in range(16):
                for zh in range(2):
                    at = (1, 2 * pair + c, x + 3, zh, points, slice(None))
                    piece = part[32 * x + 16 * zh : 32 * x + 16 * zh + 16, :]
                    ys[at] = ys[at] + (sound_timestep / 4.0) * piece

    acoustic_pack(1)
    for n in range(1, 4):
        sent.append(acoustic_send(n))
        stage_bulk(n, sound_timestep / (4 - n))
        stage_fix(n, sound_timestep / (4 - n))

    for copy in flow_copies:
        copy.wait_send()
    for copies in sent:
        for copy in copies:
            copy.wait_send()
    pltpu.make_async_copy(lists.at[pl.ds(0, ROW - 1)], lists.at[pl.ds(0, ROW - 1)], l1_s).wait()
    pltpu.make_async_copy(lists.at[rest], lists.at[rest], l2_s).wait()
    pltpu.make_async_copy(outgoing.at[others], outgoing.at[others], aa_s).wait()
    flow_out.wait()


def body(eddy, acoustic, weights, source_block, target_device, target_block, live_count):
    vmem, dma, regular = pltpu.VMEM, pltpu.SemaphoreType.DMA, pltpu.SemaphoreType.REGULAR
    anywhere = pl.BlockSpec(memory_space=pl.ANY)
    in_vmem = pl.BlockSpec(memory_space=pltpu.VMEM)
    numbers = jnp.concatenate(
        [
            target_device.reshape(1, 128),
            target_block.reshape(1, 128),
            source_block.reshape(1, 128),
            jnp.broadcast_to(live_count, (1, 128)),
        ]
    )
    return pl.pallas_call(
        kernel,
        out_shape=(
            jax.ShapeDtypeStruct(eddy.shape, F32),
            jax.ShapeDtypeStruct(acoustic.shape, F32),
        ),
        in_specs=[anywhere] * 3 + [in_vmem],
        out_specs=(anywhere, in_vmem),
        scratch_shapes=[
            vmem((5, 12, 2, FR, 128), F32),
            vmem((5, 10, 2, FR, 128), F32),
            vmem((5, 8, 32, 256), F32),
            vmem((2048 + 16, 128), F32),
            vmem((128, 128, 128), jnp.bfloat16),
            vmem((512 + 16, 128), F32),
            vmem((DEV, 8, 128), F32),
            vmem((DEV + 1, 8, 128), F32),
            vmem((4, 4, 22, 2, AR, 128), F32),
            vmem((4, 2, 12, 16, 128), F32),
            vmem((4, 2, 12, 16, 128), F32),
            vmem((4, 2, 4, 3, 2, 16, 128), F32),
            vmem((2, 20, 8, 128), F32),
            vmem((2, 20, 8, 128), F32),
            vmem((4, 16, 128), F32),
            vmem((4, 16, 128), F32),
            pltpu.SMEM((4, 128), jnp.int32),
            vmem((DEV, 2, 128), jnp.int32),
            vmem((2, DEV, 128), jnp.int32),
            vmem((2, DEV, 128), jnp.int32),
            vmem((2, 128), jnp.int32),
            pltpu.SMEM((2, 128), jnp.int32),
            vmem((512, 256), jnp.bfloat16),
            vmem((4, 512, 128), F32),
            dma((5,)), dma, dma,
            dma((2,)), dma((2,)), dma((2,)), dma((2,)), dma((4,)), dma((4,)),
            dma, dma, dma, dma, dma, dma,
            dma((4, 2)), dma((4, 2)), dma((4, 2)), dma((4, 2)), regular, regular, dma,
        ],
        compiler_params=pltpu.CompilerParams(
            collective_id=0, has_side_effects=True, vmem_limit_bytes=52 * 1024 * 1024
        ),
        name="jet_step",
    )(
        eddy,
        acoustic,
        weights.reshape(128, 128, 128),
        numbers,
    )


def solution(mesh):
    placed = (
        P(None, "gx", "row", None),
        P(None, "gx", "row", None),
        P("gx", "row", None, None, None),
        P("gx", "row", None),
        P("gx", "row", None, None),
        P("gx", "row", None),
        P("gx", "row"),
    )
    return jax.shard_map(
        body,
        mesh=mesh,
        in_specs=placed,
        out_specs=(P(None, "gx", "row", None), P(None, "gx", "row", None)),
        check_vma=False,
    )
```

```python
import functools

import jax
import jax.numpy as jnp
from jax import lax
from jax.experimental import pallas as pl
from jax.experimental.pallas import tpu as pltpu
from jax.sharding import PartitionSpec as P

MESH = pl.DeviceIdType.MESH
F32 = jnp.float32

gamma_gas = 1.4
sound_timestep = 0.5
mean_mach = 0.3
stencil = (0.75, -0.15, 1.0 / 60.0)

GX = 8
ROW = 16
DEV = GX * ROW
FR = 48
AR = 32
CORNERS = ((0, 0), (0, 1), (1, 0), (1, 1))
RADIAL = (0, 2)


def shifted(low, high, lane, step):
    if step > 0:
        a, b = pltpu.roll(low, 128 - step, 1), pltpu.roll(high, 128 - step, 1)
        keep = lane < 128 - step
    else:
        a, b = pltpu.roll(low, -step, 1), pltpu.roll(high, -step, 1)
        keep = lane >= -step
    return jnp.where(keep, a, b), jnp.where(keep, b, a)


def flow_tile(src, x, row, lane, emit):
    rows = pl.ds(row, 8)
    center = [[src[c, x, zh, rows, :] for zh in range(2)] for c in range(5)]
    upper = [shifted(center[c][0], center[c][1], lane, 1) for c in range(5)]
    lower = [shifted(center[c][0], center[c][1], lane, -1) for c in range(5)]
    for zh in range(2):
        dx, dr, dz, lap = [], [], [], []
        for c in range(5):
            xp, xm = src[c, x + 1, zh, rows, :], src[c, x - 1, zh, rows, :]
            rp, rm = src[c, x, zh, pl.ds(row + 1, 8), :], src[c, x, zh, pl.ds(row - 1, 8), :]
            zp, zm = upper[c][zh], lower[c][zh]
            dx.append(xp - xm)
            dr.append(rp - rm)
            dz.append(zp - zm)
            lap.append(((xp + xm) + (rp + rm)) + ((zp + zm) - 6.0 * center[c][zh]))
        q = [center[c][zh] for c in range(5)]
        div = dx[1] + dr[2] + dz[3]
        rho = 1.0 + q[0]
        inv = 1.0 / rho
        force = (
            rho * div,
            dx[4] * inv,
            dr[4] * inv,
            dz[4] * inv,
            (gamma_gas * q[4] + 1.0) * div,
        )
        new = []
        for c in range(5):
            adv = q[1] * dx[c] + q[2] * dr[c] + q[3] * dz[c]
            new.append(q[c] + 0.1 * (lap[c] - adv - force[c]))
        emit(zh, new)


def rate_tile(src, x, row, lane):
    rows = pl.ds(row, 8)

    def grad_x(c, zh):
        total = None
        for k in range(3):
            part = stencil[k] * (src[c, x + 4 + k, zh, rows, :] - src[c, x + 2 - k, zh, rows, :])
            total = part if total is None else total + part
        return total

    def grad_r(c, zh):
        total = None
        for k in range(3):
            part = stencil[k] * (
                src[c, x + 3, zh, pl.ds(row + k + 1, 8), :]
                - src[c, x + 3, zh, pl.ds(row - k - 1, 8), :]
            )
            total = part if total is None else total + part
        return total

    def grad_z(c):
        low, high = src[c, x + 3, 0, rows, :], src[c, x + 3, 1, rows, :]
        total = None
        for k in range(3):
            up = shifted(low, high, lane, k + 1)
            down = shifted(low, high, lane, -k - 1)
            part = [stencil[k] * (up[zh] - down[zh]) for zh in range(2)]
            total = part if total is None else [total[zh] + part[zh] for zh in range(2)]
        return total

    zp, zw = grad_z(0), grad_z(3)
    out = []
    for zh in range(2):
        xp, xu, xv, xw = (grad_x(c, zh) for c in range(4))
        out.append(
            (
                -(mean_mach * xp + xu + grad_r(2, zh) + zw[zh]),
                -(mean_mach * xu + xp),
                -(mean_mach * xv + grad_r(0, zh)),
                -(mean_mach * xw + zp[zh]),
            )
        )
    return out


def kernel(
    eddy, acoustic, weights, numbers, eddy_out, final,
    f0, f1, f2, srcs, wv, contrib, outgoing, incoming, ys, rsend, rrecv, xrecv, fsend, frecv, csend, crecv,
    numbers_s, lists, square, turned, slots, slots_s, onehot, source,
    load_sem, small_sem, slot_sem, fx_s, fx_r, fr_s, fr_r, fc_s, fc_r, l1_s, l1_r, l2_s, l2_r, aa_s, aa_r,
    ax_s, ax_r, ar_s, ar_r, plane_in, all_in, out_sem,
):
    g, r = lax.axis_index("gx"), lax.axis_index("row")
    me = g * ROW + r
    left, right = lax.rem(g + GX - 1, GX), lax.rem(g + 1, GX)
    below, above = lax.rem(r + ROW - 1, ROW), lax.rem(r + 1, ROW)
    ry, rz = lax.div(r, 4), lax.rem(r, 4)
    lane = lax.broadcasted_iota(jnp.int32, (8, 128), 1)
    sub = lax.broadcasted_iota(jnp.int32, (8, 128), 0)
    zero = jnp.zeros((8, 128), F32)

    def remote(src, dst, send, recv, where):
        return pltpu.make_async_remote_copy(
            src_ref=src, dst_ref=dst, send_sem=send, recv_sem=recv, device_id=where, device_id_type=MESH
        )

    def signal(sem, where):
        pl.semaphore_signal(sem, inc=1, device_id=where, device_id_type=MESH)

    def y_line(k):
        return g, lax.rem(ry + k, 4) * 4 + rz

    def x_line(k):
        return lax.rem(g + k, GX), r

    bar = pltpu.get_barrier_semaphore()
    for i, j in CORNERS:
        signal(bar, ((left, right)[i], (below, above)[j]))
    signal(bar, (g, below))
    signal(bar, (g, above))
    for k in range(1, 4):
        signal(bar, y_line(k))
        signal(bar, (g, ry * 4 + lax.rem(rz + k, 4)))
    for k in range(1, GX):
        signal(bar, x_line(k))

    loads = []
    for zh in range(2):
        lanes = pl.ds(128 * zh, 128)
        loads.append(
            pltpu.make_async_copy(
                eddy.at[:, :, :, lanes], f0.at[:, pl.ds(2, 8), zh, pl.ds(8, 32), :], load_sem.at[zh]
            )
        )
    for zh in range(2):
        lanes = pl.ds(128 * zh, 128)
        loads.append(
            pltpu.make_async_copy(
                acoustic.at[:, :, :, lanes],
                ys.at[0, :, pl.ds(3, 16), zh, pl.ds(8, 16), :],
                load_sem.at[2 + zh],
            )
        )
    loads.append(pltpu.make_async_copy(weights, wv, load_sem.at[4]))
    loads[0].start()
    loads[1].start()

    @pl.when(r == 0)
    def _():
        f0[:, :, :, 0:8, :] = jnp.zeros((5, 12, 2, 8, 128), F32)

    @pl.when(r == ROW - 1)
    def _():
        f0[:, :, :, 40:48, :] = jnp.zeros((5, 12, 2, 8, 128), F32)

    loads[0].wait()
    loads[1].wait()
    small = pltpu.make_async_copy(numbers, numbers_s, small_sem)
    small.start()

    flat0 = f0.reshape(5 * 12 * 2 * FR, 128)

    def flow_row(c, x, zh, row):
        return ((c * 12 + x) * 2 + zh) * FR + row

    for side in range(2):
        for c in range(5):
            for k in range(2):
                for zh in range(2):
                    start = flow_row(c, 2, zh, (8, 38)[side] + k)
                    fsend[side, (c * 2 + k) * 2 + zh] = flat0[pl.ds(start, 8, stride=2 * FR), :]
    for n, (i, j) in enumerate(CORNERS):
        for c in range(5):
            for zh in range(2):
                start = flow_row(c, (2, 9)[i], zh, (8, 39)[j])
                csend[n, 2 * c + zh : 2 * c + zh + 1, :] = flat0[pl.ds(start, 1), :]

    inner = pl.ds(8, 32)
    flow_copies = [
        remote(fsend.at[0], frecv.at[0], fr_s.at[0], fr_r.at[0], (g, below)),
        remote(fsend.at[1], frecv.at[1], fr_s.at[1], fr_r.at[1], (g, above)),
        remote(
            f0.at[:, pl.ds(2, 2), :, inner, :], f0.at[:, pl.ds(10, 2), :, inner, :],
            fx_s.at[0], fx_r.at[0], (left, r),
        ),
        remote(
            f0.at[:, pl.ds(8, 2), :, inner, :], f0.at[:, pl.ds(0, 2), :, inner, :],
            fx_s.at[1], fx_r.at[1], (right, r),
        ),
    ]
    for n, (i, j) in enumerate(CORNERS):
        where = ((left, right)[i], (below, above)[j])
        flow_copies.append(remote(csend.at[n], crecv.at[n], fc_s.at[n], fc_r.at[n], where))

    pl.semaphore_wait(bar, 4 + 2 + 6 + GX - 1)
    for copy in flow_copies[2:4] + flow_copies[:2] + flow_copies[4:]:
        copy.start()
    for copy in loads[2:]:
        copy.start()
    for k in range(1, 4):
        signal(plane_in, y_line(k))

    entry = lax.broadcasted_iota(jnp.int32, (128, 128), 0)
    device = lax.broadcasted_iota(jnp.int32, (128, 128), 1)
    named = jnp.broadcast_to(numbers[0:1, :], (128, 128)).T
    block = jnp.broadcast_to(numbers[1:2, :], (128, 128)).T
    hit = (named == device) & (entry < numbers[3:4, :])
    first = jnp.min(jnp.where(hit, entry, 128), axis=0, keepdims=True)
    last = jnp.max(jnp.where(hit, entry, -1), axis=0, keepdims=True)
    id_first = jnp.max(jnp.where(hit & (entry == first), block, -1), axis=0, keepdims=True)
    id_last = jnp.max(jnp.where(hit & (entry == last), block, -1), axis=0, keepdims=True)
    slots[0:1, :] = jnp.where(first < 128, first, 0)
    slots[1:2, :] = jnp.maximum(last, 0)
    lists[me, 0:1, :] = id_first
    lists[me, 1:2, :] = jnp.where(last > first, id_last, -1)
    slot_copy = pltpu.make_async_copy(slots, slots_s, slot_sem)
    slot_copy.start()

    @pl.loop(0, 4)
    def _(n):
        @pl.loop(0, 3)
        def _(x):
            for c in range(4):
                for zh in range(2):
                    for line in (x, x + 19):
                        for t in (8, 16):
                            ys[n, c, line, zh, t : t + 8, :] = zero

        @pl.loop(3, 19)
        def _(x):
            for c in RADIAL:
                for zh in range(2):
                    for t in (0, 24):
                        ys[n, c, x, zh, t : t + 8, :] = zero

    def clear_flow_rows(low, high):
        for row, end in ((7, r == 0), (40, r == ROW - 1)):

            @pl.when(end)
            def _():
                f1[:, low:high, :, row : row + 1, :] = jnp.zeros((5, high - low, 2, 1, 128), F32)

    def first_step(x, tiles):
        for t in tiles:
            row = 7 + 8 * t

            def emit(zh, new):
                for c in range(5):
                    f1[c, x - 1, zh, pl.ds(row, 8), :] = new[c]

            flow_tile(f0, x, row, lane, emit)

    @pl.loop(3, 9, unroll=2)
    def _(x):
        first_step(x, (1, 2, 3))

    pl.semaphore_wait(plane_in, 3)
    for k in range(1, GX):
        signal(all_in, x_line(k))

    @pl.loop(1, ROW)
    def _(k):
        remote(lists.at[me], lists.at[me], l1_s, l1_r, (g, lax.rem(r + k, ROW))).start()

    flow_copies[0].wait_recv()
    flow_copies[1].wait_recv()

    def unpack_flow(side):
        for c in range(5):
            for k in range(2):
                for zh in range(2):
                    start = flow_row(c, 2, zh, (40, 6)[side] + k)
                    flat0[pl.ds(start, 8, stride=2 * FR), :] = frecv[side, (c * 2 + k) * 2 + zh]

    @pl.when(r < ROW - 1)
    def _():
        unpack_flow(0)

    @pl.when(r > 0)
    def _():
        unpack_flow(1)

    @pl.loop(3, 9, unroll=2)
    def _(x):
        first_step(x, (0, 4))

    def second_step(x):
        for t in range(4):

            def emit(zh, new):
                for c in range(5):
                    f2[c, x, 8 * t : 8 * t + 8, 128 * zh : 128 * zh + 128] = new[c]
                rho = 1.0 + new[0]
                for c, value in enumerate((new[4], rho * new[1], rho * new[2], rho * new[3])):
                    srcs[pl.ds(8 + x * 256 + 64 * t + 4 * zh + c, 8, stride=8), :] = value

            flow_tile(f1, x + 1, 8 + 8 * t, lane, emit)

    clear_flow_rows(2, 8)

    @pl.loop(2, 6, unroll=2)
    def _(x):
        second_step(x)

    for copy in flow_copies[2:]:
        copy.wait_recv()

    flats = ys.reshape(4 * 4 * 22 * 2 * AR, 128)
    points = pl.ds(8, 16)

    def acoustic_row(n, c, x, zh, row):
        return (((n * 4 + c) * 22 + x) * 2 + zh) * AR + row

    def acoustic_pack(n):
        for side in range(2):
            for m, c in enumerate(RADIAL):
                for k in range(3):
                    for zh in range(2):
                        for half in range(2):
                            start = acoustic_row(n, c, 3 + 8 * half, zh, (8, 21)[side] + k)
                            rsend[n, side, (m * 3 + k) * 2 + zh, 8 * half : 8 * half + 8, :] = flats[
                                pl.ds(start, 8, stride=2 * AR), :
                            ]

    def acoustic_send(n):
        copies = [
            remote(rsend.at[n, 0], rrecv.at[n, 0], ar_s.at[n, 0], ar_r.at[n, 0], (g, below)),
            remote(rsend.at[n, 1], rrecv.at[n, 1], ar_s.at[n, 1], ar_r.at[n, 1], (g, above)),
            remote(
                ys.at[n, :, pl.ds(3, 3), :, points, :], xrecv.at[n, 0],
                ax_s.at[n, 0], ax_r.at[n, 0], (left, r),
            ),
            remote(
                ys.at[n, :, pl.ds(16, 3), :, points, :], xrecv.at[n, 1],
                ax_s.at[n, 1], ax_r.at[n, 1], (right, r),
            ),
        ]
        for copy in copies:
            copy.start()
        return copies

    loads[2].wait()
    loads[3].wait()
    acoustic_pack(0)
    sent = [acoustic_send(0)]

    for n, (i, j) in enumerate(CORNERS):

        @pl.when(jnp.logical_and((g < GX - 1, g > 0)[i], (r < ROW - 1, r > 0)[j]))
        def _():
            for c in range(5):
                for zh in range(2):
                    start = flow_row(c, (10, 1)[i], zh, (40, 7)[j])
                    flat0[pl.ds(start, 1), :] = crecv[n, 2 * c + zh : 2 * c + zh + 1, :]

    @pl.when(g == 0)
    def _():
        f0[:, 0:2, :, :, :] = jnp.zeros((5, 2, 2, FR, 128), F32)

    @pl.when(g == GX - 1)
    def _():
        f0[:, 10:12, :, :, :] = jnp.zeros((5, 2, 2, FR, 128), F32)

    @pl.loop(0, 4, unroll=2)
    def _(n):
        first_step(n + 1 + 6 * lax.div(n, 2), range(5))

    @pl.when(g == 0)
    def _():
        f1[:, 0, :, :, :] = jnp.zeros((5, 2, FR, 128), F32)

    @pl.when(g == GX - 1)
    def _():
        f1[:, 9, :, :, :] = jnp.zeros((5, 2, FR, 128), F32)

    clear_flow_rows(1, 2)
    clear_flow_rows(8, 9)

    @pl.loop(0, 4, unroll=2)
    def _(n):
        second_step(n + 4 * lax.div(n, 2))

    flow_out = pltpu.make_async_copy(f2, eddy_out, out_sem)
    flow_out.start()
    pltpu.make_async_copy(lists.at[pl.ds(0, ROW - 1)], lists.at[pl.ds(0, ROW - 1)], l1_r).wait()
    pl.semaphore_wait(all_in, GX - 1)
    plane = lists.at[pl.ds(g * ROW, ROW)]

    @pl.loop(1, GX)
    def _(k):
        remote(plane, plane, l2_s, l2_r, x_line(k)).start()

    loads[4].wait()
    small.wait()

    @pl.loop(0, 8, unroll=2)
    def _(m):
        for u in range(8):
            p = m * 8 + u
            low = srcs[pl.ds(8 + 4 * numbers_s[2, 2 * p], 8), :]
            high = srcs[pl.ds(4 + 4 * numbers_s[2, 2 * p + 1], 8), :]
            lhs = jnp.concatenate(
                [jnp.where(sub < 4, low, 0.0), jnp.where(sub < 4, 0.0, high)], axis=1
            ).astype(jnp.bfloat16)
            rhs = jnp.concatenate([wv[2 * p], wv[2 * p + 1]], axis=1)
            contrib[pl.ds(8 + 8 * p, 8), :] = lax.dot_general(
                lhs, rhs, (((1,), (1,)), ((), ())), preferred_element_type=F32
            )

    slot_copy.wait()

    def slot_tile(d):
        low = contrib[pl.ds(8 + 4 * jnp.clip(slots_s[0, d], 0, 127), 8), :]
        high = contrib[pl.ds(4 + 4 * jnp.clip(slots_s[1, d], 0, 127), 8), :]
        return jnp.where(sub < 4, low, high)

    @pl.loop(1, DEV, unroll=6)
    def _(k):
        d = lax.rem(me + k, DEV)
        outgoing[d] = slot_tile(d)
        where = (lax.div(d, ROW), lax.rem(d, ROW))
        remote(outgoing.at[d], incoming.at[me], aa_s, aa_r, where).start()

    incoming[me] = slot_tile(me)

    def source_tile(c, x, zh, t):
        return source[c, pl.ds(pl.multiple_of(x * 32 + zh * 16 + 8 * t, 8), 8), :]

    def stage_bulk(n, step):
        @pl.loop(0, 16, unroll=4)
        def _(x):
            for t in range(2):
                rate = rate_tile(ys.at[n], x, 8 + 8 * t, lane)
                for zh in range(2):
                    for c in range(4):
                        old = ys[0, c, x + 3, zh, 8 + 8 * t : 16 + 8 * t, :]
                        change = rate[zh][c]
                        if n > 0:
                            change = change + source_tile(c, x, zh, t)
                        new = old + step * change
                        if n < 3:
                            ys[n + 1, c, x + 3, zh, 8 + 8 * t : 16 + 8 * t, :] = new
                        else:
                            final[c, x, 8 * t : 8 * t + 8, 128 * zh : 128 * zh + 128] = new

    def halo_share(lines, ell, upper):
        total = None
        for k in range(ell + 1, 4):
            part = stencil[k - 1] * (lines[k - ell - 1] if upper else lines[ell - k + 3])
            total = part if total is None else total + part
        return total if upper else -total

    def fix_x(n, step, side):
        for zh in range(2):
            for t in range(2):
                rows = pl.ds(8 * t, 8)
                halo = [[xrecv[n, side, c, k, zh, rows, :] for k in range(3)] for c in range(4)]
                for ell in range(3):
                    x = ell if side else 15 - ell
                    gp, gu, gv, gw = (halo_share(halo[c], ell, side == 0) for c in range(4))
                    changes = (mean_mach * gp + gu, mean_mach * gu + gp, mean_mach * gv, mean_mach * gw)
                    for c in range(4):
                        if n < 3:
                            at = (n + 1, c, x + 3, zh, pl.ds(8 + 8 * t, 8), slice(None))
                            ys[at] = ys[at] - step * changes[c]
                        else:
                            at = (c, x, rows, pl.ds(128 * zh, 128))
                            final[at] = final[at] - step * changes[c]

    def clear_ends(n):
        @pl.when(r == ROW - 1)
        def _():
            rrecv[n, 0] = jnp.zeros((12, 16, 128), F32)

        @pl.when(r == 0)
        def _():
            rrecv[n, 1] = jnp.zeros((12, 16, 128), F32)

    def fix_r(n, step):
        for side in range(2):
            for zh in range(2):
                for half in range(2):
                    eight = pl.ds(8 * half, 8)
                    halo = [
                        [rrecv[n, side, (m * 3 + k) * 2 + zh, eight, :] for k in range(3)] for m in range(2)
                    ]
                    for ell in range(3):
                        row = ell if side else 15 - ell
                        for m, c in enumerate(RADIAL):
                            change = step * halo_share(halo[1 - m], ell, side == 0)
                            start = acoustic_row(n + 1, c, 3 + 8 * half, zh, 8 + row)
                            at = pl.ds(start, 8, stride=2 * AR)
                            new = flats[at, :] - change
                            flats[at, :] = new
                            if n > 0:
                                k = ell if side else 2 - ell
                                rsend[n + 1, 1 - side, (m * 3 + k) * 2 + zh, eight, :] = new

    def fix_r_last(n, step):
        for side in range(2):
            for m, c in enumerate(RADIAL):
                for k in range(3):
                    for zh in range(2):
                        for half in range(2):
                            start = acoustic_row(n, c, 3 + 8 * half, zh, (24, 5)[side] + k)
                            flats[pl.ds(start, 8, stride=2 * AR), :] = rrecv[
                                n, side, (m * 3 + k) * 2 + zh, 8 * half : 8 * half + 8, :
                            ]

        @pl.loop(0, 16, unroll=4)
        def _(x):
            for side in range(2):
                for zh in range(2):
                    for m, c in enumerate(RADIAL):
                        other = RADIAL[1 - m]
                        total = None
                        for k in range(1, 4):
                            if side:
                                part = jnp.where(sub < k, ys[n, other, x + 3, zh, pl.ds(8 - k, 8), :], 0.0)
                                part = (-step * stencil[k - 1]) * part
                            else:
                                part = jnp.where(sub >= 8 - k, ys[n, other, x + 3, zh, pl.ds(16 + k, 8), :], 0.0)
                                part = (step * stencil[k - 1]) * part
                            total = part if total is None else total + part
                        at = (c, x, pl.ds(0 if side else 8, 8), pl.ds(128 * zh, 128))
                        final[at] = final[at] - total

    def stage_fix(n, step):
        sent[n][2].wait_recv()
        sent[n][3].wait_recv()

        @pl.when(g < GX - 1)
        def _():
            fix_x(n, step, 0)

        @pl.when(g > 0)
        def _():
            fix_x(n, step, 1)

        sent[n][0].wait_recv()
        sent[n][1].wait_recv()
        clear_ends(n)
        if n < 3:
            fix_r(n, step)
        else:
            fix_r_last(n, step)

    stage_bulk(0, sound_timestep / 4.0)
    stage_fix(0, sound_timestep / 4.0)

    rest = pl.ds(0, DEV - ROW)
    pltpu.make_async_copy(lists.at[rest], lists.at[rest], l2_r).wait()

    @pl.loop(0, DEV, unroll=8)
    def _(j):
        for k in range(2):
            square[k, pl.ds(j, 1), :] = lists[j, k : k + 1, :]

    for k in range(2):
        turned[k] = square[k].T
    ids = [turned[k, pl.ds(me, 1), :] for k in range(2)]

    @pl.loop(0, 16)
    def _(x):
        place = lax.broadcasted_iota(jnp.int32, (32, 128), 0)
        place = (x * 16 + lax.rem(place, 16)) * 2 + lax.div(place, 16)
        for k in range(2):
            onehot[pl.ds(pl.multiple_of(x * 32, 32), 32), 128 * k : 128 * k + 128] = jnp.where(
                place == ids[k], 1.0, 0.0
            ).astype(jnp.bfloat16)

    others = pl.ds(0, DEV - 1)
    pltpu.make_async_copy(incoming.at[others], incoming.at[others], aa_r).wait()

    flat_in = incoming.reshape((DEV + 1) * 8, 128)
    for pair in range(2):
        value = jnp.concatenate(
            [
                jnp.concatenate(
                    [flat_in[pl.ds(4 * k + 2 * pair + c, DEV, stride=8), :] for k in range(2)], axis=0
                )
                for c in range(2)
            ],
            axis=1,
        )
        high = value.astype(jnp.bfloat16)
        low = (value - high.astype(F32)).astype(jnp.bfloat16)

        rows = onehot[...]
        total = jnp.dot(rows, high, preferred_element_type=F32) + jnp.dot(
            rows, low, preferred_element_type=F32
        )
        for c in range(2):
            part = total[:, 128 * c : 128 * c + 128]
            source[2 * pair + c] = part
            for x in range(16):
                for zh in range(2):
                    at = (1, 2 * pair + c, x + 3, zh, points, slice(None))
                    piece = part[32 * x + 16 * zh : 32 * x + 16 * zh + 16, :]
                    ys[at] = ys[at] + (sound_timestep / 4.0) * piece

    acoustic_pack(1)
    for n in range(1, 4):
        sent.append(acoustic_send(n))
        stage_bulk(n, sound_timestep / (4 - n))
        stage_fix(n, sound_timestep / (4 - n))

    for copy in flow_copies:
        copy.wait_send()
    for copies in sent:
        for copy in copies:
            copy.wait_send()
    pltpu.make_async_copy(lists.at[pl.ds(0, ROW - 1)], lists.at[pl.ds(0, ROW - 1)], l1_s).wait()
    pltpu.make_async_copy(lists.at[rest], lists.at[rest], l2_s).wait()
    pltpu.make_async_copy(outgoing.at[others], outgoing.at[others], aa_s).wait()
    flow_out.wait()


def body(eddy, acoustic, weights, source_block, target_device, target_block, live_count):
    vmem, dma, regular = pltpu.VMEM, pltpu.SemaphoreType.DMA, pltpu.SemaphoreType.REGULAR
    anywhere = pl.BlockSpec(memory_space=pl.ANY)
    in_vmem = pl.BlockSpec(memory_space=pltpu.VMEM)
    numbers = jnp.concatenate(
        [
            target_device.reshape(1, 128),
            target_block.reshape(1, 128),
            source_block.reshape(1, 128),
            jnp.broadcast_to(live_count, (1, 128)),
        ]
    )
    return pl.pallas_call(
        kernel,
        out_shape=(
            jax.ShapeDtypeStruct(eddy.shape, F32),
            jax.ShapeDtypeStruct(acoustic.shape, F32),
        ),
        in_specs=[anywhere] * 3 + [in_vmem],
        out_specs=(anywhere, in_vmem),
        scratch_shapes=[
            vmem((5, 12, 2, FR, 128), F32),
            vmem((5, 10, 2, FR, 128), F32),
            vmem((5, 8, 32, 256), F32),
            vmem((2048 + 16, 128), F32),
            vmem((128, 128, 128), jnp.bfloat16),
            vmem((512 + 16, 128), F32),
            vmem((DEV, 8, 128), F32),
            vmem((DEV + 1, 8, 128), F32),
            vmem((4, 4, 22, 2, AR, 128), F32),
            vmem((4, 2, 12, 16, 128), F32),
            vmem((4, 2, 12, 16, 128), F32),
            vmem((4, 2, 4, 3, 2, 16, 128), F32),
            vmem((2, 20, 8, 128), F32),
            vmem((2, 20, 8, 128), F32),
            vmem((4, 16, 128), F32),
            vmem((4, 16, 128), F32),
            pltpu.SMEM((4, 128), jnp.int32),
            vmem((DEV, 2, 128), jnp.int32),
            vmem((2, DEV, 128), jnp.int32),
            vmem((2, DEV, 128), jnp.int32),
            vmem((2, 128), jnp.int32),
            pltpu.SMEM((2, 128), jnp.int32),
            vmem((512, 256), jnp.bfloat16),
            vmem((4, 512, 128), F32),
            dma((5,)), dma, dma,
            dma((2,)), dma((2,)), dma((2,)), dma((2,)), dma((4,)), dma((4,)),
            dma, dma, dma, dma, dma, dma,
            dma((4, 2)), dma((4, 2)), dma((4, 2)), dma((4, 2)), regular, regular, dma,
        ],
        compiler_params=pltpu.CompilerParams(
            collective_id=0, has_side_effects=True, vmem_limit_bytes=52 * 1024 * 1024
        ),
        name="jet_step",
    )(
        eddy,
        acoustic,
        weights.reshape(128, 128, 128),
        numbers,
    )


def solution(mesh):
    placed = (
        P(None, "gx", "row", None),
        P(None, "gx", "row", None),
        P("gx", "row", None, None, None),
        P("gx", "row", None),
        P("gx", "row", None, None),
        P("gx", "row", None),
        P("gx", "row"),
    )
    return jax.shard_map(
        body,
        mesh=mesh,
        in_specs=placed,
        out_specs=(P(None, "gx", "row", None), P(None, "gx", "row", None)),
        check_vma=False,
    )
```
